256 devices in a mesh: dp: 64 (over y, x, z_hi, core), tensor: 4 (over z_lo).
Axes of the slice: x: 4, y: 4, z: 8 (z_hi: 2, z_lo: 4; z = z_hi * 4 + z_lo), core: 2. Of those that a mesh axis runs over, the one named last changes fastest.
Arguments:
- inputs: bfloat16 [32768, 5120], P('dp', 'tensor'), may hold values from -6 to 6
- out_grads: bfloat16 [32768, 27648], P('dp', 'tensor'), may hold values from -6 to 6
- query_inputs: bfloat16 [8192, 5120], P('dp', 'tensor'), may hold values from -6 to 6
- query_grads: bfloat16 [8192, 27648], P('dp', 'tensor'), may hold values from -6 to 6
- in_proj: bfloat16 [5120, 64], P('tensor'), may hold values from -0.078125 to 0.078125
- out_proj: bfloat16 [27648, 64], P('tensor'), may hold values from -0.0390625 to 0.0390625
- doc_ids: int32 [64, 512], P('dp'), may hold values from 0 to 15, never falling along the last dimension, each value on 1 to 64 neighbouring positions
- query_ids: int32 [64, 128], P('dp'), may hold values from 0 to 1, never falling along the last dimension, each value on 1 to 96 neighbouring positions
Outputs:
- scores: float32 [1024, 128], P('dp')
The draws below stay inside these ranges and needn't reach their ends.
Inputs may be any that keep to these rules, and one draw needn't show every extreme that they name: `doc_ids`: in each row the numbers never fall, and each of the 16 documents has 1 to 64 tokens, one exactly 64. `query_ids`: in each row the numbers never fall, and each of the 2 query documents has 1 to 96 tokens.
All inputs are finite; a program needn't handle non-finite values.
Results may differ from the reference program's by a relative error of at most 0.0046.
Values sent between devices are 32-bit elements; how exact they have to be, the bound alone decides.
A program may use at most 128 MiB of HBM per device.

```python
import math
import jax
import jax.numpy as jnp
import numpy as np
from jax import lax

D = 5120
FF = 27648
PROJ = 64
VEC = 4096
TOK_DEV = 512
QTOK_DEV = 128
DOCS_DEV = 16
QDOCS_DEV = 2
ITERS = 3
DOC_MOST = 64
QDOC_MOST = 96
GROUPS = 64
TOKENS = 32768
QTOKENS = 8192


def levels(key, extent, split, least, high):
    gain, own = 1.0, jax.random.fold_in(key, 6)
    for axis_at, shards_of in split:
        steps = jnp.exp(jax.random.uniform(jax.random.fold_in(own, axis_at), (shards_of,), jnp.float32, least / len(split), high / len(split)))
        gain = gain * jnp.repeat(steps, extent[axis_at] // shards_of).reshape([-1 if axis == axis_at else 1 for axis in range(len(extent))])
    return gain


def length_profile(amount, total, bound, slope):
    loads = [(1 << 20) // math.isqrt(standing ** slope) + 1 for standing in range(2, amount + 1)]
    surplus, holding = total - bound - (amount - 1), [1] * (amount - 1)
    while surplus > 0:
        movable = [i for i in range(amount - 1) if holding[i] < bound]
        whole, budget = sum([loads[i] for i in movable]), surplus
        for i in movable:
            addition = min(bound - holding[i], max(1, budget * loads[i] // whole), surplus)
            holding[i] = holding[i] + addition
            surplus = surplus - addition
    return np.array([bound] + holding)


def ragged_sizes(own_key, count, total, limit, skew):
    if count == 2:
        one = jax.random.randint(own_key, (), max(1, total - limit), min(limit, total - 1) + 1)
        return jnp.stack([one, total - one])
    lengths = jnp.asarray(length_profile(count, total, limit, skew), jnp.int32)
    couples = (count - 1) // 2
    giver, receiver = lengths[1:1 + 2 * couples:2], lengths[2:2 + 2 * couples:2]
    margin = jnp.minimum(giver - 1, limit - receiver)
    moved = jax.random.randint(jax.random.fold_in(own_key, 1), (couples,), 0, 1 << 20) % (margin + 1)
    lengths = lengths.at[1:1 + 2 * couples:2].set(giver - moved).at[2:2 + 2 * couples:2].set(receiver + moved)
    return lengths[jax.random.permutation(jax.random.fold_in(own_key, 2), count)]


def centred(rng, extent, scale, reach, pieces=(), kind=jnp.bfloat16):
    entries = scale * jax.random.normal(rng, extent, jnp.float32)
    if pieces:
        entries = entries * levels(rng, extent, pieces, -0.22, 0.18)
    return jnp.clip(entries, -reach, reach).astype(kind)


def setup_inputs(seed: int = 0) -> dict:
    keys = jax.random.split(jax.random.key(seed), 9)
    inputs = centred(keys[0], (TOKENS, D), 1.0, 6.0, ((0, 64), (1, 4)))
    out_grads = centred(keys[1], (TOKENS, FF), 1.0, 6.0, ((0, 64), (1, 4)))
    query_inputs = centred(keys[2], (QTOKENS, D), 1.0, 6.0, ((0, 64), (1, 4)))
    query_grads = centred(keys[3], (QTOKENS, FF), 1.0, 6.0, ((0, 64), (1, 4)))
    in_proj = centred(keys[4], (D, PROJ), D ** -0.5, 0.078125, ((0, 4),))
    out_proj = centred(keys[5], (FF, PROJ), FF ** -0.5, 0.0390625, ((0, 4),))
    doc_ids = jax.vmap(lambda own: jnp.searchsorted(jnp.cumsum(ragged_sizes(own, DOCS_DEV, TOK_DEV, DOC_MOST, 2)), jnp.arange(TOK_DEV), side="right"))(jax.random.split(keys[6], GROUPS)).reshape((GROUPS, TOK_DEV)).astype(jnp.int32)
    query_ids = jax.vmap(lambda own: jnp.searchsorted(jnp.cumsum(ragged_sizes(own, QDOCS_DEV, QTOK_DEV, QDOC_MOST, 2)), jnp.arange(QTOK_DEV), side="right"))(jax.random.split(keys[7], GROUPS)).reshape((GROUPS, QTOK_DEV)).astype(jnp.int32)
    return {"inputs": inputs, "out_grads": out_grads, "query_inputs": query_inputs, "query_grads": query_grads, "in_proj": in_proj, "out_proj": out_proj, "doc_ids": doc_ids, "query_ids": query_ids}


damping = 0.1


def kron_rows(left, right):
    return (left[:, :, None] * right[:, None, :]).reshape(left.shape[0], -1).astype(jnp.bfloat16)


def group_sums(kron, ids, count):
    groups = ids.shape[0]
    blocks = kron.reshape(groups, -1, kron.shape[1])

    def single(pair):
        block_kron, row_ids = pair
        onehot = (row_ids[:, None] == jnp.arange(count, dtype=jnp.int32)[None, :]).astype(jnp.bfloat16)
        return jnp.dot(onehot.T, block_kron, preferred_element_type=jnp.float32)

    return lax.map(single, (blocks, ids)).reshape(groups * count, -1)


def reference(inputs, out_grads, query_inputs, query_grads, in_proj, out_proj, doc_ids, query_ids):
    highest = lax.Precision.HIGHEST
    in_feats = jnp.dot(inputs, in_proj, preferred_element_type=jnp.float32)
    out_feats = jnp.dot(out_grads, out_proj, preferred_element_type=jnp.float32)
    query_in = jnp.dot(query_inputs, in_proj, preferred_element_type=jnp.float32)
    query_out = jnp.dot(query_grads, out_proj, preferred_element_type=jnp.float32)
    kron = kron_rows(in_feats, out_feats)
    query_kron = kron_rows(query_in, query_out)
    doc_grads = group_sums(kron, doc_ids, DOCS_DEV)
    query_vecs = group_sums(query_kron, query_ids, QDOCS_DEV)
    kron_wide = kron.astype(jnp.float32)

    def apply(direction):
        inner = jnp.dot(kron_wide, direction, precision=highest)
        return jnp.dot(kron_wide.T, inner, precision=highest) / TOKENS + damping * direction

    target = query_vecs.T
    solution = jnp.zeros_like(target)
    residual = target
    direction = target
    norms_now = jnp.sum(residual * residual, axis=0)
    for sweep in range(ITERS):
        image = apply(direction)
        curvature = jnp.sum(direction * image, axis=0)
        step_size = norms_now / curvature
        solution = solution + step_size * direction
        residual = residual - step_size * image
        if sweep + 1 < ITERS:
            norms_next = jnp.sum(residual * residual, axis=0)
            direction = residual + (norms_next / norms_now) * direction
            norms_now = norms_next
    return jnp.dot(doc_grads, solution, precision=highest) / VEC
```

```python
import functools

import jax
import jax.numpy as jnp
from jax import lax
from jax.experimental import pallas as pl
from jax.experimental.pallas import tpu as pltpu
from jax.sharding import PartitionSpec as P

MESH = pl.DeviceIdType.MESH
F32, BF16 = jnp.float32, jnp.bfloat16
NT = (((1,), (1,)), ((), ()))
ITERS = 3
DAMPING = 0.1
TILES = 8


def split_bf16(value):
    high = value.astype(BF16)
    return high, (value - high.astype(F32)).astype(BF16)


def query_sum(value):
    return jnp.sum(jnp.sum(value, axis=1), axis=1, keepdims=True)


def kernel(
    tokens_all,
    inp, outg, qinp, qoutg, win, wout, ids, qids,
    out,
    win_v, wout_v, inp_v, outg_v, qinp_v, qoutg_v,
    part, qpart, rs, qrs, ft, rhs1, rhs2, feat_a, lhs, wbuf, acc,
    direction, residual, usend, urecv, rbuf, ssend, srecv, fsend, frecv, order,
    load_sem, rs_send, rs_recv, q_send, q_recv, ring_send, ring_recv, sib_send, sib_recv,
    b_send, b_recv, u_send, u_recv, r_send, r_recv, s_send, s_recv, f_send, f_recv,
):
    dp = lax.axis_index("dp")
    zl = lax.axis_index("tensor")
    core = lax.rem(dp, 2)
    half = lax.rem(dp // 2, 2)
    xy = dp // 4
    xpos = lax.rem(xy, 4)
    ypos = xy // 4
    z = half * 4 + zl
    spot = z * 2 + core

    def plane(index):
        return (index * 4 + half * 2 + core, zl)

    def column(zpos, which):
        return (xy * 4 + (zpos // 4) * 2 + which, lax.rem(zpos, 4))

    def chunk_of(zpos, which):
        return ((zpos // 4) * 2 + which) * 4 + lax.rem(zpos, 4)

    def remote(src, dst, send, recv, device):
        return pltpu.make_async_remote_copy(
            src_ref=src, dst_ref=dst, send_sem=send, recv_sem=recv, device_id=device, device_id_type=MESH
        )

    loads = [
        pltpu.make_async_copy(win, win_v, load_sem.at[0]),
        pltpu.make_async_copy(qinp, qinp_v, load_sem.at[1]),
        pltpu.make_async_copy(wout, wout_v, load_sem.at[2]),
        pltpu.make_async_copy(qoutg, qoutg_v, load_sem.at[3]),
    ]
    for load in loads:
        load.start()

    def chunk_loads(owner):
        rows = pl.ds(pl.multiple_of(owner * 128, 128), 128)
        return (
            pltpu.make_async_copy(inp.at[rows, :], inp_v.at[owner], load_sem.at[4 + owner]),
            pltpu.make_async_copy(outg.at[rows, :], outg_v.at[owner], load_sem.at[8 + owner]),
        )

    for step in range(4):
        for load in chunk_loads(lax.rem(zl + 1 + step, 4)):
            load.start()

    barrier = pltpu.get_barrier_semaphore()

    def greet(step, carry):
        pl.semaphore_signal(barrier, inc=1, device_id=plane(lax.rem(xy + step, 16)), device_id_type=MESH)
        other = lax.rem(spot + step, 16)
        pl.semaphore_signal(
            barrier, inc=1, device_id=column(other // 2, lax.rem(other, 2)), device_id_type=MESH
        )
        return carry

    lax.fori_loop(1, 16, greet, 0)

    for load in loads:
        load.wait()

    def project(left, right):
        return jnp.concatenate(
            [
                jnp.dot(left, win_v[...], preferred_element_type=F32),
                jnp.dot(right, wout_v[...], preferred_element_type=F32),
            ],
            axis=1,
        )

    qpart[...] = project(qinp_v[...], qoutg_v[...])
    pl.semaphore_wait(barrier, 30)
    diag = lax.rem(xpos + ypos, 4)
    query_owner = jnp.where(core == 0, diag, 3 - diag)
    slot = jnp.where(core == 0, zl, 3 - zl)
    owns = zl == query_owner
    q_copy = remote(qpart, qrs.at[zl], q_send, q_recv.at[zl], (dp, query_owner))

    @pl.when(jnp.logical_not(owns))
    def _():
        q_copy.start()

    def rs_copy(owner):
        return remote(part.at[owner], rs.at[zl], rs_send.at[owner], rs_recv.at[zl], (dp, owner))

    def project_chunk(step, carry):
        owner = lax.rem(zl + 1 + step, 4)
        for load in chunk_loads(owner):
            load.wait()
        part[owner] = project(inp_v[owner], outg_v[owner])

        @pl.when(step < 3)
        def _():
            rs_copy(owner).start()

        return carry

    lax.fori_loop(0, 4, project_chunk, 0)

    def b_copy(target):
        rows = pl.ds(pl.multiple_of(ypos * 64, 64), 64)
        return remote(
            direction.at[rows, :], direction.at[rows, :], b_send.at[target], b_recv.at[ypos], plane(target)
        )

    lane = lax.broadcasted_iota(jnp.int32, (128, 128), 1)

    @pl.when(owns)
    def _():
        qrs[zl] = qpart[...]
        for step in range(1, 4):
            source = lax.rem(zl + step, 4)
            remote(qpart, qrs.at[source], q_send, q_recv.at[source], (dp, source)).wait_recv()
        feats = (qrs[0] + qrs[1]) + (qrs[2] + qrs[3])
        turned = feats.T
        right = jnp.concatenate(
            [jnp.where(lane < 64, pltpu.roll(feats, 64, 1), 0.0), jnp.where(lane >= 64, feats, 0.0)], axis=0
        )
        rows = []
        for doc in range(2):
            mask = (qids[...] == doc).astype(F32)
            rows.append(jnp.concatenate([turned[0:32] * mask, turned[32:64] * mask], axis=1))
        left = jnp.concatenate(rows, axis=0)
        direction[pl.ds(pl.multiple_of(ypos * 64, 64), 64), :] = jnp.dot(
            left, right, precision=lax.Precision.HIGHEST, preferred_element_type=F32
        )

        def spread(step, carry):
            b_copy(lax.rem(xy + step, 16)).start()
            return carry

        lax.fori_loop(1, 16, spread, 0)

    rs[zl] = part[zl]
    for step in range(1, 4):
        source = lax.rem(zl + step, 4)
        remote(part.at[source], rs.at[source], rs_send.at[source], rs_recv.at[source], (dp, source)).wait_recv()
    feats = (rs[0] + rs[1]) + (rs[2] + rs[3])
    own = chunk_of(z, core)
    ids_own = jnp.zeros((1, 128), F32)
    for index in range(4):
        ids_own = ids_own + jnp.where(zl == index, ids[:, index * 128 : (index + 1) * 128].astype(F32), 0.0)
    ft[own, 0:128] = feats.T
    ft[own, 128:136] = jnp.broadcast_to(ids_own, (8, 128))

    pieces = (pl.ds(0, 64), pl.ds(64, 72))
    reach = ((4, 3), (3, 4))

    def ring_copy(way, piece, step):
        sign = 1 if way == 0 else 7
        origin = lax.rem(z + 8 * 8 - (sign if way == 0 else -1) * (step - 1), 8)
        where = ft.at[chunk_of(origin, core), pieces[piece], :]
        return remote(
            where, where, ring_send.at[way, piece, step], ring_recv.at[way, piece, step],
            column(lax.rem(z + sign, 8), core),
        )

    def ring_arrival(way, piece, step):
        origin = lax.rem(z + 8 - step, 8) if way == 0 else lax.rem(z + step, 8)
        where = ft.at[chunk_of(origin, core), pieces[piece], :]
        return remote(
            where, where, ring_send.at[way, piece, step], ring_recv.at[way, piece, step],
            column(lax.rem(z + 1, 8), core),
        )

    def sibling_copy(offset, piece, which):
        origin = lax.rem(z + offset, 8)
        where = ft.at[chunk_of(origin, which), pieces[piece], :]
        return remote(
            where, where, sib_send.at[offset, piece], sib_recv.at[offset, piece], column(z, 1 - core)
        )

    for step in range(1, 5):
        for way in range(2):
            for piece in range(2):
                if step > 1 and step - 1 <= reach[way][piece]:
                    ring_arrival(way, piece, step - 1).wait_recv()
                if step <= reach[way][piece]:
                    ring_copy(way, piece, step).start()
        for piece in range(2):
            if step == 1:
                sibling_copy(0, piece, core).start()
            else:
                for way in range(2):
                    if step - 1 <= reach[way][piece]:
                        offset = (8 - (step - 1)) if way == 0 else (step - 1)
                        sibling_copy(offset, piece, core).start()
    for way in range(2):
        for piece in range(2):
            if reach[way][piece] == 4:
                ring_arrival(way, piece, 4).wait_recv()
                sibling_copy(4, piece, core).start()
    for offset in range(8):
        for piece in range(2):
            sibling_copy(offset, piece, 1 - core).wait_recv()

    for source in range(4):
        @pl.when(jnp.logical_not(jnp.logical_and(owns, ypos == source)))
        def _():
            rows = pl.ds(source * 64, 64)
            remote(
                direction.at[rows, :], direction.at[rows, :], b_send.at[0], b_recv.at[source], plane(xy)
            ).wait_recv()

    def prepare(tile, carry):
        both = jnp.concatenate([ft[2 * tile], ft[2 * tile + 1]], axis=1)
        feat_a[tile] = both[0:64]
        high, low = split_bf16(both[64:128])
        zero = jnp.zeros_like(high)
        rhs1[tile] = jnp.concatenate([high, high, low, low], axis=0)
        rhs2[tile] = jnp.concatenate(
            [
                jnp.concatenate([high, zero, low, zero], axis=0),
                jnp.concatenate([zero, high, zero, low], axis=0),
            ],
            axis=1,
        )
        return carry

    lax.fori_loop(0, TILES, prepare, 0)

    lane_row = lax.broadcasted_iota(jnp.int32, (256, 128), 1)
    own_rows = pl.ds(pl.multiple_of(xy * 16, 16), 16)
    query_row = lax.broadcasted_iota(jnp.int32, (8, 1), 0)
    residual[...] = direction[...]
    norms = None
    steps = []
    for sweep in range(ITERS):
        last = sweep == ITERS - 1
        vector = direction[...]
        high = vector.astype(BF16).astype(F32)
        low = vector - high
        first = jnp.where(lane_row < 64, high, pltpu.roll(low, 64, 1)).astype(BF16)
        second = jnp.where(lane_row < 64, pltpu.roll(high, 64, 1), low).astype(BF16)
        lhs[0:256, 0:128] = first
        lhs[0:256, 128:256] = first
        lhs[256:512, 0:128] = second
        lhs[256:512, 128:256] = second
        if not last:
            acc[...] = jnp.zeros_like(acc)

        def product(tile, squares):
            made = jnp.dot(lhs[...], rhs1[tile], preferred_element_type=F32)
            left = feat_a[tile].reshape(2, 1, 32, 256)
            inner = jnp.sum(jnp.sum(made.reshape(2, 8, 32, 256) * left, axis=0), axis=1)
            wbuf[tile, sweep * 8 : sweep * 8 + 8] = inner
            if not last:
                spread = (inner.reshape(1, 8, 1, 256) * left).reshape(2, 256, 256)
                for group in (0, 1):
                    hi, lo = split_bf16(spread[group])
                    right = rhs2[tile, :, group * 256 : (group + 1) * 256]
                    acc[...] += lax.dot_general(hi, right, NT, preferred_element_type=F32)
                    acc[...] += lax.dot_general(lo, right, NT, preferred_element_type=F32)
            square = inner * inner
            return squares + square[:, 0:128] + square[:, 128:256]

        squares = lax.fori_loop(0, TILES, product, jnp.zeros((8, 128), F32))
        cube = vector.reshape(8, 32, 128)
        power = query_sum(cube * cube)
        if sweep == 0:
            norms = power
        if not last:
            image = acc[:, 0:128] + acc[:, 128:256]
            usend[:, 0:16] = image.reshape(16, 16, 128)
            usend[:, 16:24] = jnp.broadcast_to(squares[None], (16, 8, 128))
            urecv[sweep, xy] = usend[xy]

            def u_copy(target, source):
                return remote(
                    usend.at[target], urecv.at[sweep, source], u_send.at[sweep, target],
                    u_recv.at[sweep, source], plane(target),
                )

            def u_start(step, carry):
                u_copy(lax.rem(xy + step, 16), xy).start()
                return carry

            def u_wait(step, carry):
                other = lax.rem(xy + step, 16)
                u_copy(other, other).wait_recv()
                return carry

            def u_done(step, carry):
                u_copy(lax.rem(xy + step, 16), xy).wait_send()
                return carry

            lax.fori_loop(1, 16, u_start, 0)
            lax.fori_loop(1, 16, u_wait, 0)
            total = jnp.sum(urecv[sweep], axis=0)
            squared = jnp.sum(total[16:24], axis=1, keepdims=True)
            step_size = norms / (squared / tokens_all + DAMPING * power)
            steps.append(step_size)
            mine = jnp.sum(jnp.where(query_row == xy // 2, step_size, 0.0), axis=0, keepdims=True)
            own_image = total[0:16] / tokens_all + DAMPING * direction[own_rows, :]
            rbuf[sweep, own_rows, :] = residual[own_rows, :] - mine * own_image

            def r_copy(target, source):
                rows = pl.ds(pl.multiple_of(source * 16, 16), 16)
                return remote(
                    rbuf.at[sweep, rows, :], rbuf.at[sweep, rows, :], r_send.at[sweep, target],
                    r_recv.at[sweep, source], plane(target),
                )

            def r_start(step, carry):
                r_copy(lax.rem(xy + step, 16), xy).start()
                return carry

            def r_wait(step, carry):
                other = lax.rem(xy + step, 16)
                r_copy(other, other).wait_recv()
                return carry

            lax.fori_loop(1, 16, r_start, 0)
            lax.fori_loop(1, 16, r_wait, 0)
            lax.fori_loop(1, 16, u_done, 0)
            left_over = rbuf[sweep]
            residual[...] = left_over
            cube_r = left_over.reshape(8, 32, 128)
            norms_next = query_sum(cube_r * cube_r)
            ratio = norms_next / norms
            direction_next = cube_r + ratio.reshape(8, 1, 1) * cube
            if sweep == 0:
                @pl.when(owns)
                def _():
                    def b_done(step, carry):
                        b_copy(lax.rem(xy + step, 16)).wait_send()
                        return carry

                    lax.fori_loop(1, 16, b_done, 0)

            direction[...] = direction_next.reshape(256, 128)
            norms = norms_next

    ssend[...] = squares
    srecv[xy] = squares

    def s_copy(target, source):
        return remote(ssend, srecv.at[source], s_send.at[target], s_recv.at[source], plane(target))

    def s_start(step, carry):
        s_copy(lax.rem(xy + step, 16), xy).start()
        return carry

    def s_wait(step, carry):
        other = lax.rem(xy + step, 16)
        s_copy(other, other).wait_recv()
        return carry

    lax.fori_loop(1, 16, s_start, 0)

    doc_row = lax.broadcasted_iota(jnp.int32, (128, 128), 0).astype(F32)
    sums = []
    for group in range(4):
        onehot = jnp.concatenate(
            [(doc_row == ft[group * 4 + index, 128:129]).astype(BF16) for index in range(4)], axis=1
        )
        hi, lo = split_bf16(jnp.concatenate([wbuf[2 * group], wbuf[2 * group + 1]], axis=1))
        sums.append(
            lax.dot_general(hi, onehot, NT, preferred_element_type=F32)
            + lax.dot_general(lo, onehot, NT, preferred_element_type=F32)
        )

    lax.fori_loop(1, 16, s_wait, 0)
    squared = jnp.sum(jnp.sum(srecv[...], axis=0), axis=1, keepdims=True)
    steps.append(norms / (squared / tokens_all + DAMPING * power))

    for group in range(4):
        scores = steps[0] * sums[group][0:8] + steps[1] * sums[group][8:16] + steps[2] * sums[group][16:24]
        fsend[group] = scores * (1.0 / 4096)

    def f_slot(zpos, which):
        other = lax.rem(zpos, 4)
        return (jnp.where(which == 0, other, 3 - other) * 2 + zpos // 4) * 2 + which

    frecv[f_slot(z, core)] = fsend[half * 2 + core]

    def f_copy(step, back):
        other = lax.rem(spot + step, 16)
        zpos, which = other // 2, lax.rem(other, 2)
        landing = f_slot(zpos, which) if back else f_slot(z, core)
        return remote(
            fsend.at[(zpos // 4) * 2 + which], frecv.at[landing], f_send.at[step], f_recv.at[landing],
            column(zpos, which),
        )

    def f_start(step, carry):
        f_copy(step, False).start()
        return carry

    def f_wait(step, carry):
        f_copy(step, True).wait_recv()
        return carry

    lax.fori_loop(1, 16, f_start, 0)
    lax.fori_loop(1, 16, f_wait, 0)
    for where in range(16):
        diagonal, rest = where // 4, where % 4
        for row in range(4):
            begin = row * 32 + ((diagonal - row) % 4) * 8 + rest * 2
            order[begin : begin + 2] = frecv[where, 2 * row : 2 * row + 2]
    out[...] = order[...].T[0:16]

    @pl.when(jnp.logical_not(owns))
    def _():
        q_copy.wait_send()

    for step in range(3):
        rs_copy(lax.rem(zl + 1 + step, 4)).wait_send()
    for way in range(2):
        for piece in range(2):
            for step in range(1, reach[way][piece] + 1):
                ring_copy(way, piece, step).wait_send()
    for offset in range(8):
        for piece in range(2):
            sibling_copy(offset, piece, core).wait_send()

    def finish(step, carry):
        other = lax.rem(xy + step, 16)
        for sweep in range(ITERS - 1):
            rows = pl.ds(pl.multiple_of(xy * 16, 16), 16)
            remote(
                rbuf.at[sweep, rows, :], rbuf.at[sweep, rows, :], r_send.at[sweep, other],
                r_recv.at[sweep, xy], plane(other),
            ).wait_send()
        s_copy(other, xy).wait_send()
        f_copy(step, False).wait_send()
        return carry

    lax.fori_loop(1, 16, finish, 0)


def local(inputs, out_grads, query_inputs, query_grads, in_proj, out_proj, doc_ids, query_ids):
    tokens_all = inputs.shape[0] * lax.axis_size("dp")
    hbm = pl.BlockSpec(memory_space=pl.ANY)
    vmem = pl.BlockSpec(memory_space=pltpu.VMEM)
    dma = pltpu.SemaphoreType.DMA
    return pl.pallas_call(
        functools.partial(kernel, float(tokens_all)),
        out_shape=jax.ShapeDtypeStruct((16, 128), F32),
        in_specs=[hbm] * 6 + [vmem] * 2,
        out_specs=vmem,
        scratch_shapes=[
            pltpu.VMEM((1280, 64), BF16),
            pltpu.VMEM((6912, 64), BF16),
            pltpu.VMEM((4, 128, 1280), BF16),
            pltpu.VMEM((4, 128, 6912), BF16),
            pltpu.VMEM((128, 1280), BF16),
            pltpu.VMEM((128, 6912), BF16),
            pltpu.VMEM((4, 128, 128), F32),
            pltpu.VMEM((128, 128), F32),
            pltpu.VMEM((4, 128, 128), F32),
            pltpu.VMEM((4, 128, 128), F32),
            pltpu.VMEM((16, 136, 128), F32),
            pltpu.VMEM((TILES, 256, 256), BF16),
            pltpu.VMEM((TILES, 256, 512), BF16),
            pltpu.VMEM((TILES, 64, 256), F32),
            pltpu.VMEM((512, 256), BF16),
            pltpu.VMEM((TILES, 24, 256), F32),
            pltpu.VMEM((256, 256), F32),
            pltpu.VMEM((256, 128), F32),
            pltpu.VMEM((256, 128), F32),
            pltpu.VMEM((16, 24, 128), F32),
            pltpu.VMEM((2, 16, 24, 128), F32),
            pltpu.VMEM((2, 256, 128), F32),
            pltpu.VMEM((8, 128), F32),
            pltpu.VMEM((16, 8, 128), F32),
            pltpu.VMEM((4, 8, 128), F32),
            pltpu.VMEM((16, 8, 128), F32),
            pltpu.VMEM((128, 128), F32),
            dma((12,)),
            dma((4,)),
            dma((4,)),
            dma,
            dma((4,)),
            dma((2, 2, 5)),
            dma((2, 2, 5)),
            dma((8, 2)),
            dma((8, 2)),
            dma((16,)),
            dma((4,)),
            dma((2, 16)),
            dma((2, 16)),
            dma((2, 16)),
            dma((2, 16)),
            dma((16,)),
            dma((16,)),
            dma((16,)),
            dma((16,)),
        ],
        compiler_params=pltpu.CompilerParams(
            collective_id=0, has_side_effects=True, vmem_limit_bytes=48 * 1024 * 1024
        ),
    )(inputs, out_grads, query_inputs, query_grads, in_proj, out_proj, doc_ids, query_ids)


def solution(mesh):
    return jax.shard_map(
        local,
        mesh=mesh,
        in_specs=(
            P("dp", "tensor"),
            P("dp", "tensor"),
            P("dp", "tensor"),
            P("dp", "tensor"),
            P("tensor", None),
            P("tensor", None),
            P("dp", None),
            P("dp", None),
        ),
        out_specs=P("dp", None),
        check_vma=False,
    )
```

```python
import functools

import jax
import jax.numpy as jnp
from jax import lax
from jax.experimental import pallas as pl
from jax.experimental.pallas import tpu as pltpu
from jax.sharding import PartitionSpec as P

MESH = pl.DeviceIdType.MESH
F32, BF16 = jnp.float32, jnp.bfloat16
NT = (((1,), (1,)), ((), ()))
ITERS = 3
DAMPING = 0.1
TILES = 8


def split_bf16(value):
    high = value.astype(BF16)
    return high, (value - high.astype(F32)).astype(BF16)


def query_sum(value):
    return jnp.sum(jnp.sum(value, axis=1), axis=1, keepdims=True)


def kernel(
    tokens_all,
    inp, outg, qinp, qoutg, win, wout, ids_in, qids_in,
    out,
    ids, qids, win_v, wout_v, inp_v, outg_v, qinp_v, qoutg_v,
    part, qpart, rs, qrs, ft, rhs1, rhs2, feat_a, lhs, wbuf, acc, onehot,
    direction, residual, usend, urecv, rbuf, ssend, srecv, fsend, frecv, order,
    load_sem, rs_send, rs_recv, q_send, q_recv, ag_send, ag_recv, sib_send, sib_recv,
    b_send, b_recv, u_send, u_recv, r_send, r_recv, s_send, s_recv, f_send, f_recv,
):
    dp = lax.axis_index("dp")
    zl = lax.axis_index("tensor")
    low = lax.rem(dp, 4)
    core = lax.rem(dp, 2)
    half = low // 2
    xy = dp // 4
    xpos = lax.rem(xy, 4)
    ypos = xy // 4
    z = half * 4 + zl
    pending = []

    plane = [(lax.rem(xy + step, 16), (lax.rem(dp + 4 * step, 64), zl)) for step in range(1, 16)]
    lows = [low] + [lax.rem(low + step, 4) for step in range(1, 4)]
    zls = [zl] + [lax.rem(zl + step, 4) for step in range(1, 4)]
    column = [(lows[a], zls[b], (dp - low + lows[a], zls[b])) for a in range(4) for b in range(4) if a or b]

    barrier = pltpu.get_barrier_semaphore()
    for index in range(15):
        for device in (plane[index][1], column[index][2]):
            pl.semaphore_signal(barrier, inc=1, device_id=device, device_id_type=MESH)

    def up_column(offset, which=None):
        zpos = lax.rem(z + offset, 8)
        return (xy * 4 + (zpos // 4) * 2 + (core if which is None else which), lax.rem(zpos, 4))

    def remote(src, dst, send, recv, device):
        return pltpu.make_async_remote_copy(
            src_ref=src, dst_ref=dst, send_sem=send, recv_sem=recv, device_id=device, device_id_type=MESH
        )

    loads = [
        pltpu.make_async_copy(win, win_v, load_sem.at[0]),
        pltpu.make_async_copy(qinp, qinp_v, load_sem.at[1]),
        pltpu.make_async_copy(wout, wout_v, load_sem.at[2]),
        pltpu.make_async_copy(qoutg, qoutg_v, load_sem.at[3]),
        pltpu.make_async_copy(ids_in, ids, load_sem.at[12]),
        pltpu.make_async_copy(qids_in, qids, load_sem.at[13]),
    ]
    owners = [zls[2], zls[1], zls[3], zl]
    chunk_loads = []
    for step in range(4):
        rows = pl.ds(pl.multiple_of(owners[step] * 128, 128), 128)
        chunk_loads.append(
            (
                pltpu.make_async_copy(inp.at[rows, :], inp_v.at[step], load_sem.at[4 + step]),
                pltpu.make_async_copy(outg.at[rows, :], outg_v.at[step], load_sem.at[8 + step]),
            )
        )
    for load in loads:
        load.start()
    for step in range(2):
        for load in chunk_loads[step]:
            load.start()

    def project(left, right):
        return jnp.concatenate(
            [
                lax.dot_general(left, win_v[...], NT, preferred_element_type=F32),
                lax.dot_general(right, wout_v[...], NT, preferred_element_type=F32),
            ],
            axis=1,
        )

    def project_chunk(step):
        for load in chunk_loads[step]:
            load.wait()
        part[step] = project(inp_v[step], outg_v[step])

    rs_copies = [
        remote(part.at[step], rs.at[zl], rs_send.at[step], rs_recv.at[zl], (dp, owners[step])) for step in range(3)
    ]
    diag = lax.rem(xpos + ypos, 4)
    query_owner = jnp.where(core == 0, diag, 3 - diag)
    owns = zl == query_owner
    q_copy = remote(qpart, qrs.at[zl], q_send, q_recv.at[zl], (dp, query_owner))

    for load in loads:
        load.wait()
    for step in range(2, 4):
        for load in chunk_loads[step]:
            load.start()
    qpart[...] = project(qinp_v[...], qoutg_v[...])
    project_chunk(0)
    pl.semaphore_wait(barrier, 30)

    @pl.when(jnp.logical_not(owns))
    def _():
        q_copy.start()

    rs_copies[0].start()
    for step in range(1, 3):
        project_chunk(step)
        rs_copies[step].start()
    project_chunk(3)
    rs[zl] = part[3]

    def first_done():
        @pl.when(jnp.logical_not(owns))
        def _():
            q_copy.wait_send()

        for copy in rs_copies:
            copy.wait_send()

    pending.append(first_done)

    lane = lax.broadcasted_iota(jnp.int32, (128, 128), 1)
    pair_rows = pl.ds(pl.multiple_of(ypos * 64, 64), 64)
    b_copies = [
        remote(direction.at[pair_rows, :], direction.at[pair_rows, :], b_send.at[index], b_recv.at[ypos], device)
        for index, (_, device) in enumerate(plane)
    ]

    @pl.when(owns)
    def _():
        qrs[zl] = qpart[...]
        for step in range(1, 4):
            remote(qpart, qrs.at[zls[step]], q_send, q_recv.at[zls[step]], (dp, zls[step])).wait_recv()
        feats = (qrs[0] + qrs[1]) + (qrs[2] + qrs[3])
        turned = feats.T
        right = jnp.concatenate(
            [jnp.where(lane < 64, pltpu.roll(feats, 64, 1), 0.0), jnp.where(lane >= 64, feats, 0.0)], axis=0
        )
        rows = []
        for doc in range(2):
            mask = (qids[...] == doc).astype(F32)
            rows.append(jnp.concatenate([turned[0:32] * mask, turned[32:64] * mask], axis=1))
        direction[pair_rows, :] = jnp.dot(
            jnp.concatenate(rows, axis=0), right, precision=lax.Precision.HIGHEST, preferred_element_type=F32
        )
        for copy in b_copies:
            copy.start()

    ids_own = jnp.zeros((1, 128), F32)
    for index in range(4):
        ids_own = ids_own + jnp.where(zl == index, ids[:, index * 128 : (index + 1) * 128].astype(F32), 0.0)
    own = z * 2 + core
    ft[own, 128:136] = jnp.broadcast_to(ids_own, (8, 128))
    for step in range(1, 4):
        remote(part.at[0], rs.at[zls[step]], rs_send.at[0], rs_recv.at[zls[step]], (dp, zls[step])).wait_recv()
    ft[own, 0:128] = ((rs[0] + rs[1]) + (rs[2] + rs[3])).T

    whole, upper, lower = pl.ds(0, 136), pl.ds(0, 64), pl.ds(64, 72)

    def handed(index, origin, rows, target):
        where = ft.at[lax.rem(z + origin, 8) * 2 + core, rows, :]
        return remote(where, where, ag_send.at[index], ag_recv.at[index], up_column(target))

    def sibling(index, origin, rows, back=False):
        where = ft.at[lax.rem(z + origin, 8) * 2 + (1 - core if back else core), rows, :]
        return remote(where, where, sib_send.at[index], sib_recv.at[index], up_column(0, 1 - core))

    arrivals = ((6, whole), (2, whole), (7, whole), (1, whole), (5, whole), (3, whole), (4, upper), (4, lower))
    sent = []

    def start(copy):
        copy.start()
        sent.append(copy)

    start(handed(0, 0, whole, 2))
    start(handed(1, 0, whole, 6))
    start(handed(2, 0, whole, 1))
    start(handed(3, 0, whole, 7))
    start(sibling(8, 0, whole))

    def arrive(index):
        origin, rows = arrivals[index]
        handed(index, origin, rows, 1).wait_recv()

    def pass_on(index):
        origin, rows = arrivals[index]
        start(sibling(index, origin, rows))

    arrive(0)
    start(handed(4, 6, whole, 1))
    start(handed(6, 6, upper, 2))
    pass_on(0)
    arrive(1)
    start(handed(5, 2, whole, 7))
    start(handed(7, 2, lower, 6))
    pass_on(1)
    for index in (2, 3):
        arrive(index)
        pass_on(index)

    def prepare(tile):
        both = jnp.concatenate([ft[2 * tile], ft[2 * tile + 1]], axis=1)
        feat_a[tile] = both[0:64]
        high, rest = split_bf16(both[64:128])
        zero = jnp.zeros_like(high)
        rhs1[tile] = jnp.concatenate([high, high, rest, rest], axis=0)
        rhs2[tile] = jnp.concatenate(
            [
                jnp.concatenate([high, zero, rest, zero], axis=0),
                jnp.concatenate([zero, high, zero, rest], axis=0),
            ],
            axis=1,
        )

    def sibling_tile(index, origin, rows=whole):
        sibling(index, origin, rows, True).wait_recv()

    near = [(8, 0), (0, 6), (1, 2), (2, 7), (3, 1)]
    for index, origin in near:
        sibling_tile(index, origin)
        prepare(lax.rem(z + origin, 8))

    for source in range(4):
        @pl.when(jnp.logical_not(jnp.logical_and(owns, ypos == source)))
        def _():
            rows = pl.ds(source * 64, 64)
            remote(
                direction.at[rows, :], direction.at[rows, :], b_send.at[0], b_recv.at[source], plane[0][1]
            ).wait_recv()

    lane_row = lax.broadcasted_iota(jnp.int32, (256, 128), 1)
    own_rows = pl.ds(pl.multiple_of(xy * 16, 16), 16)
    query_row = lax.broadcasted_iota(jnp.int32, (8, 1), 0)
    doc_row = lax.broadcasted_iota(jnp.int32, (128, 128), 0).astype(F32)

    def set_lhs(vector):
        high = vector.astype(BF16).astype(F32)
        rest = vector - high
        first = jnp.where(lane_row < 64, high, pltpu.roll(rest, 64, 1)).astype(BF16)
        second = jnp.where(lane_row < 64, pltpu.roll(high, 64, 1), rest).astype(BF16)
        lhs[0:256, 0:128] = first
        lhs[0:256, 128:256] = first
        lhs[256:512, 0:128] = second
        lhs[256:512, 128:256] = second

    def product(tile, squares, fresh, back):
        made = jnp.dot(lhs[...], rhs1[tile], preferred_element_type=F32)
        left = feat_a[tile].reshape(2, 1, 32, 256)
        inner = jnp.sum(jnp.sum(made.reshape(2, 8, 32, 256) * left, axis=0), axis=1)
        wbuf[tile] = inner
        if back:
            spread = (inner.reshape(1, 8, 1, 256) * left).reshape(2, 256, 256).astype(BF16)
            image = lax.dot_general(
                jnp.concatenate([spread[0], spread[1]], axis=1), rhs2[tile], NT, preferred_element_type=F32
            )
            if fresh:
                acc[...] = image
            else:
                acc[...] += image
        square = inner * inner
        return squares + square[:, 0:128] + square[:, 128:256]

    def document_sums():
        sums = []
        for group in range(4):
            side = pl.ds((group % 2) * 128, 128)
            tiles = [wbuf[(group // 2) * 4 + index, :, side] for index in range(4)]
            every = jnp.concatenate(tiles, axis=1)
            high = every.astype(BF16).astype(F32)
            both = jnp.concatenate([high, every - high], axis=0).astype(BF16)
            made = lax.dot_general(both, onehot[group], NT, preferred_element_type=F32)
            sums.append(made[0:8] + made[8:16])
        return sums

    def send_all(copies):
        for copy in copies:
            copy.start()

    def sent_all(copies):
        for copy in copies:
            copy.wait_send()

    residual[...] = direction[...]
    norms = None
    scores = None
    for sweep in range(ITERS):
        last = sweep == ITERS - 1
        vector = direction[...]
        set_lhs(vector)
        squares = jnp.zeros((8, 128), F32)
        if sweep == 0:
            for place, (_, origin) in enumerate(near):
                squares = product(lax.rem(z + origin, 8), squares, place == 0, True)
            for index in range(4, 8):
                arrive(index)
                pass_on(index)
            sibling_tile(4, 5)
            prepare(lax.rem(z + 5, 8))
            sibling_tile(5, 3)
            prepare(lax.rem(z + 3, 8))
            sibling_tile(6, 4, upper)
            sibling_tile(7, 4, lower)
            prepare(lax.rem(z + 4, 8))
            for origin in (5, 3, 4):
                squares = product(lax.rem(z + origin, 8), squares, False, True)
        else:
            for tile in range(TILES):
                squares = product(tile, squares, tile == 0, not last)
        cube = vector.reshape(8, 32, 128)
        if not last:
            image = acc[:, 0:128] + acc[:, 128:256]
            usend[:, 0:16] = image.reshape(16, 16, 128)
            usend[:, 16:24] = jnp.broadcast_to(squares[None], (16, 8, 128))
            u_copies = [
                remote(usend.at[target], urecv.at[sweep, xy], u_send.at[sweep, index], u_recv.at[sweep, xy], device)
                for index, (target, device) in enumerate(plane)
            ]
            send_all(u_copies)
            urecv[sweep, xy] = usend[xy]
            if sweep == 0:
                for group in range(4):
                    for index in range(4):
                        chunk = ((group // 2) * 4 + index) * 2 + group % 2
                        onehot[group, :, index * 128 : (index + 1) * 128] = (doc_row == ft[chunk, 128:129]).astype(BF16)
            sums = document_sums()
            power = query_sum(cube * cube)
            if sweep == 0:
                norms = power
            for source, device in plane:
                remote(
                    usend.at[0], urecv.at[sweep, source], u_send.at[sweep, 0], u_recv.at[sweep, source], device
                ).wait_recv()
            total = jnp.sum(urecv[sweep], axis=0)
            squared = jnp.sum(total[16:24], axis=1, keepdims=True)
            step_size = norms / (squared / tokens_all + DAMPING * power)
            mine = jnp.sum(jnp.where(query_row == xy // 2, step_size, 0.0), axis=0, keepdims=True)
            own_image = total[0:16] / tokens_all + DAMPING * direction[own_rows, :]
            rbuf[sweep, own_rows, :] = residual[own_rows, :] - mine * own_image
            r_copies = [
                remote(
                    rbuf.at[sweep, own_rows, :], rbuf.at[sweep, own_rows, :], r_send.at[sweep, index],
                    r_recv.at[sweep, xy], device,
                )
                for index, (_, device) in enumerate(plane)
            ]
            send_all(r_copies)
            pending.append(functools.partial(sent_all, r_copies))
            terms = [step_size * value for value in sums]
            scores = terms if scores is None else [a + b for a, b in zip(scores, terms)]
            sent_all(u_copies)
            if sweep == 0:
                @pl.when(owns)
                def _():
                    sent_all(b_copies)

            for source, device in plane:
                rows = pl.ds(pl.multiple_of(source * 16, 16), 16)
                remote(
                    rbuf.at[sweep, rows, :], rbuf.at[sweep, rows, :], r_send.at[sweep, 0],
                    r_recv.at[sweep, source], device,
                ).wait_recv()
            left_over = rbuf[sweep]
            residual[...] = left_over
            cube_r = left_over.reshape(8, 32, 128)
            norms_next = query_sum(cube_r * cube_r)
            ratio = norms_next / norms
            direction[...] = (cube_r + ratio.reshape(8, 1, 1) * cube).reshape(256, 128)
            norms = norms_next

    ssend[...] = squares
    s_copies = [
        remote(ssend, srecv.at[xy], s_send.at[index], s_recv.at[xy], device)
        for index, (_, device) in enumerate(plane)
    ]
    send_all(s_copies)
    pending.append(functools.partial(sent_all, s_copies))
    srecv[xy] = squares
    power = query_sum(cube * cube)
    sums = document_sums()
    for source, device in plane:
        remote(ssend, srecv.at[source], s_send.at[0], s_recv.at[source], device).wait_recv()
    squared = jnp.sum(jnp.sum(srecv[...], axis=0), axis=1, keepdims=True)
    step_size = norms / (squared / tokens_all + DAMPING * power)

    for group in range(4):
        fsend[group] = (scores[group] + step_size * sums[group]) * (1.0 / 4096)

    def f_slot(where, height):
        return jnp.where(lax.rem(where, 2) == 0, height, 3 - height) * 4 + where

    own_slot = f_slot(low, zl)
    f_copies = [
        remote(fsend.at[where], frecv.at[own_slot], f_send.at[index], f_recv.at[own_slot], device)
        for index, (where, _, device) in enumerate(column)
    ]
    send_all(f_copies)
    pending.append(functools.partial(sent_all, f_copies))
    frecv[own_slot] = fsend[low]
    for copy in sent:
        copy.wait_send()
    for done in pending:
        done()
    for where, height, device in column:
        slot = f_slot(where, height)
        remote(fsend.at[0], frecv.at[slot], f_send.at[0], f_recv.at[slot], device).wait_recv()
    for where in range(16):
        diagonal, rest = where // 4, where % 4
        for row in range(4):
            begin = row * 32 + ((diagonal - row) % 4) * 8 + rest * 2
            order[begin : begin + 2] = frecv[where, 2 * row : 2 * row + 2]
    out[...] = order[...].T[0:16]


def local(inputs, out_grads, query_inputs, query_grads, in_proj, out_proj, doc_ids, query_ids):
    tokens_all = inputs.shape[0] * lax.axis_size("dp")
    hbm = pl.BlockSpec(memory_space=pltpu.HBM)
    vmem = pl.BlockSpec(memory_space=pltpu.VMEM)
    dma = pltpu.SemaphoreType.DMA
    return pl.pallas_call(
        functools.partial(kernel, float(tokens_all)),
        out_shape=jax.ShapeDtypeStruct((16, 128), F32),
        in_specs=[hbm] * 8,
        out_specs=vmem,
        scratch_shapes=[
            pltpu.VMEM((1, 512), jnp.int32),
            pltpu.VMEM((1, 128), jnp.int32),
            pltpu.VMEM((64, 1280), BF16),
            pltpu.VMEM((64, 6912), BF16),
            pltpu.VMEM((4, 128, 1280), BF16),
            pltpu.VMEM((4, 128, 6912), BF16),
            pltpu.VMEM((128, 1280), BF16),
            pltpu.VMEM((128, 6912), BF16),
            pltpu.VMEM((4, 128, 128), F32),
            pltpu.VMEM((128, 128), F32),
            pltpu.VMEM((4, 128, 128), F32),
            pltpu.VMEM((4, 128, 128), F32),
            pltpu.VMEM((16, 136, 128), F32),
            pltpu.VMEM((TILES, 256, 256), BF16),
            pltpu.VMEM((TILES, 256, 512), BF16),
            pltpu.VMEM((TILES, 64, 256), F32),
            pltpu.VMEM((512, 256), BF16),
            pltpu.VMEM((TILES, 8, 256), F32),
            pltpu.VMEM((256, 256), F32),
            pltpu.VMEM((4, 128, 512), BF16),
            pltpu.VMEM((256, 128), F32),
            pltpu.VMEM((256, 128), F32),
            pltpu.VMEM((16, 24, 128), F32),
            pltpu.VMEM((2, 16, 24, 128), F32),
            pltpu.VMEM((2, 256, 128), F32),
            pltpu.VMEM((8, 128), F32),
            pltpu.VMEM((16, 8, 128), F32),
            pltpu.VMEM((4, 8, 128), F32),
            pltpu.VMEM((16, 8, 128), F32),
            pltpu.VMEM((128, 128), F32),
            dma((14,)),
            dma((4,)),
            dma((4,)),
            dma,
            dma((4,)),
            dma((8,)),
            dma((8,)),
            dma((9,)),
            dma((9,)),
            dma((16,)),
            dma((4,)),
            dma((2, 16)),
            dma((2, 16)),
            dma((2, 16)),
            dma((2, 16)),
            dma((16,)),
            dma((16,)),
            dma((16,)),
            dma((16,)),
        ],
        compiler_params=pltpu.CompilerParams(
            collective_id=0, has_side_effects=True, vmem_limit_bytes=62 * 1024 * 1024
        ),
    )(inputs, out_grads, query_inputs, query_grads, in_proj.T, out_proj.T, doc_ids, query_ids)


def solution(mesh):
    return jax.shard_map(
        local,
        mesh=mesh,
        in_specs=(
            P("dp", "tensor"),
            P("dp", "tensor"),
            P("dp", "tensor"),
            P("dp", "tensor"),
            P("tensor", None),
            P("tensor", None),
            P("dp", None),
            P("dp", None),
        ),
        out_specs=P("dp", None),
        check_vma=False,
    )
```

```python
import functools

import jax
import jax.numpy as jnp
from jax import lax
from jax.experimental import pallas as pl
from jax.experimental.pallas import tpu as pltpu
from jax.sharding import PartitionSpec as P

MESH = pl.DeviceIdType.MESH
F32, BF16 = jnp.float32, jnp.bfloat16
NT = (((1,), (1,)), ((), ()))
ITERS = 3
DAMPING = 0.1
TILES = 8


def split_bf16(value):
    high = value.astype(BF16)
    return high, (value - high.astype(F32)).astype(BF16)


def query_sum(value):
    return jnp.sum(jnp.sum(value, axis=1), axis=1, keepdims=True)


def kernel(
    tokens_all,
    inp, outg, qinp, qoutg, win, wout, ids_in, qids_in,
    out,
    ids, qids, win_v, wout_v, inp_v, outg_v, qinp_v, qoutg_v,
    part, qpart, rs, qrs, ft, rhs1, rhs2, feat_a, lhs, wbuf, acc, onehot,
    direction, residual, usend, urecv, rbuf, ssend, srecv, fsend, frecv, order,
    load_sem, rs_send, rs_recv, q_send, q_recv, ag_send, ag_recv, sib_send, sib_recv,
    b_send, b_recv, u_send, u_recv, r_send, r_recv, s_send, s_recv, f_send, f_recv,
):
    dp = lax.axis_index("dp")
    zl = lax.axis_index("tensor")
    low = lax.rem(dp, 4)
    core = lax.rem(dp, 2)
    half = low // 2
    xy = dp // 4
    xpos = lax.rem(xy, 4)
    ypos = xy // 4
    z = half * 4 + zl
    pending = []

    plane = [(lax.rem(xy + step, 16), (lax.rem(dp + 4 * step, 64), zl)) for step in range(1, 16)]
    lows = [low] + [lax.rem(low + step, 4) for step in range(1, 4)]
    zls = [zl] + [lax.rem(zl + step, 4) for step in range(1, 4)]
    column = [(lows[a], zls[b], (dp - low + lows[a], zls[b])) for a in range(4) for b in range(4) if a or b]

    barrier = pltpu.get_barrier_semaphore()
    for index in range(15):
        for device in (plane[index][1], column[index][2]):
            pl.semaphore_signal(barrier, inc=1, device_id=device, device_id_type=MESH)

    def up_column(offset, which=None):
        zpos = lax.rem(z + offset, 8)
        return (xy * 4 + (zpos // 4) * 2 + (core if which is None else which), lax.rem(zpos, 4))

    def remote(src, dst, send, recv, device):
        return pltpu.make_async_remote_copy(
            src_ref=src, dst_ref=dst, send_sem=send, recv_sem=recv, device_id=device, device_id_type=MESH
        )

    loads = [
        pltpu.make_async_copy(win, win_v, load_sem.at[0]),
        pltpu.make_async_copy(qinp, qinp_v, load_sem.at[1]),
        pltpu.make_async_copy(wout, wout_v, load_sem.at[2]),
        pltpu.make_async_copy(qoutg, qoutg_v, load_sem.at[3]),
        pltpu.make_async_copy(ids_in, ids, load_sem.at[12]),
        pltpu.make_async_copy(qids_in, qids, load_sem.at[13]),
    ]
    owners = [zls[2], zls[1], zls[3], zl]
    chunk_loads = []
    for step in range(4):
        rows = pl.ds(pl.multiple_of(owners[step] * 128, 128), 128)
        chunk_loads.append(
            (
                pltpu.make_async_copy(inp.at[rows, :], inp_v.at[step], load_sem.at[4 + step]),
                pltpu.make_async_copy(outg.at[rows, :], outg_v.at[step], load_sem.at[8 + step]),
            )
        )
    loads[0].start()
    loads[2].start()
    for pair in chunk_loads:
        for load in pair:
            load.start()
    for index in (1, 3, 4, 5):
        loads[index].start()

    def project(left, right):
        return jnp.concatenate(
            [
                lax.dot_general(left, win_v[...], NT, preferred_element_type=F32),
                lax.dot_general(right, wout_v[...], NT, preferred_element_type=F32),
            ],
            axis=1,
        )

    def project_chunk(step):
        for load in chunk_loads[step]:
            load.wait()
        part[step] = project(inp_v[step], outg_v[step])

    rs_copies = [
        remote(part.at[step], rs.at[zl], rs_send.at[step], rs_recv.at[zl], (dp, owners[step])) for step in range(3)
    ]
    diag = lax.rem(xpos + ypos, 4)
    query_owner = jnp.where(core == 0, diag, 3 - diag)
    owns = zl == query_owner
    q_copy = remote(qpart, qrs.at[zl], q_send, q_recv.at[zl], (dp, query_owner))

    loads[0].wait()
    loads[2].wait()
    project_chunk(0)
    project_chunk(1)
    pl.semaphore_wait(barrier, 30)
    rs_copies[0].start()
    rs_copies[1].start()
    project_chunk(2)
    rs_copies[2].start()
    for index in (1, 3, 4, 5):
        loads[index].wait()
    qpart[...] = project(qinp_v[...], qoutg_v[...])

    @pl.when(jnp.logical_not(owns))
    def _():
        q_copy.start()

    project_chunk(3)
    rs[zl] = part[3]

    def first_done():
        @pl.when(jnp.logical_not(owns))
        def _():
            q_copy.wait_send()

        for copy in rs_copies:
            copy.wait_send()

    pending.append(first_done)

    ids_own = jnp.zeros((1, 128), F32)
    for index in range(4):
        ids_own = ids_own + jnp.where(zl == index, ids[:, index * 128 : (index + 1) * 128].astype(F32), 0.0)
    own = z * 2 + core
    ft[own, 128:136] = jnp.broadcast_to(ids_own, (8, 128))
    for step in range(1, 4):
        remote(part.at[0], rs.at[zls[step]], rs_send.at[0], rs_recv.at[zls[step]], (dp, zls[step])).wait_recv()
    ft[own, 0:128] = ((rs[0] + rs[1]) + (rs[2] + rs[3])).T

    whole, upper, lower = pl.ds(0, 136), pl.ds(0, 64), pl.ds(64, 72)

    def handed(index, origin, rows, target):
        where = ft.at[lax.rem(z + origin, 8) * 2 + core, rows, :]
        return remote(where, where, ag_send.at[index], ag_recv.at[index], up_column(target))

    def sibling(index, origin, rows, back=False):
        where = ft.at[lax.rem(z + origin, 8) * 2 + (1 - core if back else core), rows, :]
        return remote(where, where, sib_send.at[index], sib_recv.at[index], up_column(0, 1 - core))

    arrivals = ((6, whole), (2, whole), (7, whole), (1, whole), (5, whole), (3, whole), (4, upper), (4, lower))
    sent = []

    def start(copy):
        copy.start()
        sent.append(copy)

    start(handed(0, 0, whole, 2))
    start(handed(1, 0, whole, 6))
    start(handed(2, 0, whole, 1))
    start(handed(3, 0, whole, 7))
    start(sibling(8, 0, whole))

    lane = lax.broadcasted_iota(jnp.int32, (128, 128), 1)
    pair_rows = pl.ds(pl.multiple_of(ypos * 64, 64), 64)
    b_copies = [
        remote(direction.at[pair_rows, :], direction.at[pair_rows, :], b_send.at[index], b_recv.at[ypos], device)
        for index, (_, device) in enumerate(plane)
    ]

    @pl.when(owns)
    def _():
        qrs[zl] = qpart[...]
        for step in range(1, 4):
            remote(qpart, qrs.at[zls[step]], q_send, q_recv.at[zls[step]], (dp, zls[step])).wait_recv()
        feats = (qrs[0] + qrs[1]) + (qrs[2] + qrs[3])
        turned = feats.T
        right = jnp.concatenate(
            [jnp.where(lane < 64, pltpu.roll(feats, 64, 1), 0.0), jnp.where(lane >= 64, feats, 0.0)], axis=0
        )
        rows = []
        for doc in range(2):
            mask = (qids[...] == doc).astype(F32)
            rows.append(jnp.concatenate([turned[0:32] * mask, turned[32:64] * mask], axis=1))
        direction[pair_rows, :] = jnp.dot(
            jnp.concatenate(rows, axis=0), right, precision=lax.Precision.HIGHEST, preferred_element_type=F32
        )
        for copy in b_copies:
            copy.start()

    def arrive(index):
        origin, rows = arrivals[index]
        handed(index, origin, rows, 1).wait_recv()

    def pass_on(index):
        origin, rows = arrivals[index]
        start(sibling(index, origin, rows))

    arrive(0)
    start(handed(4, 6, whole, 1))
    start(handed(6, 6, upper, 2))
    pass_on(0)
    arrive(1)
    start(handed(5, 2, whole, 7))
    start(handed(7, 2, lower, 6))
    pass_on(1)
    for index in (2, 3):
        arrive(index)
        pass_on(index)

    def prepare(tile):
        both = jnp.concatenate([ft[2 * tile], ft[2 * tile + 1]], axis=1)
        feat_a[tile] = both[0:64]
        high, rest = split_bf16(both[64:128])
        zero = jnp.zeros_like(high)
        rhs1[tile] = jnp.concatenate([high, high, rest, rest], axis=0)
        rhs2[tile] = jnp.concatenate(
            [
                jnp.concatenate([high, zero, rest, zero], axis=0),
                jnp.concatenate([zero, high, zero, rest], axis=0),
            ],
            axis=1,
        )

    def sibling_tile(index, origin, rows=whole):
        sibling(index, origin, rows, True).wait_recv()

    near = [(8, 0), (0, 6), (1, 2), (2, 7), (3, 1)]
    for index, origin in near:
        sibling_tile(index, origin)
        prepare(lax.rem(z + origin, 8))

    for source in range(4):
        @pl.when(jnp.logical_not(jnp.logical_and(owns, ypos == source)))
        def _():
            rows = pl.ds(source * 64, 64)
            remote(
                direction.at[rows, :], direction.at[rows, :], b_send.at[0], b_recv.at[source], plane[0][1]
            ).wait_recv()

    lane_row = lax.broadcasted_iota(jnp.int32, (256, 128), 1)
    own_rows = pl.ds(pl.multiple_of(xy * 16, 16), 16)
    query_row = lax.broadcasted_iota(jnp.int32, (8, 1), 0)
    doc_row = lax.broadcasted_iota(jnp.int32, (128, 128), 0).astype(F32)

    def set_lhs(vector):
        high = vector.astype(BF16).astype(F32)
        rest = vector - high
        first = jnp.where(lane_row < 64, high, pltpu.roll(rest, 64, 1)).astype(BF16)
        second = jnp.where(lane_row < 64, pltpu.roll(high, 64, 1), rest).astype(BF16)
        lhs[0:256, 0:128] = first
        lhs[0:256, 128:256] = first
        lhs[256:512, 0:128] = second
        lhs[256:512, 128:256] = second

    def product(tile, squares, fresh, back):
        made = jnp.dot(lhs[...], rhs1[tile], preferred_element_type=F32)
        left = feat_a[tile].reshape(2, 1, 32, 256)
        inner = jnp.sum(jnp.sum(made.reshape(2, 8, 32, 256) * left, axis=0), axis=1)
        wbuf[tile] = inner
        if back:
            spread = (inner.reshape(1, 8, 1, 256) * left).reshape(2, 256, 256).astype(BF16)
            image = lax.dot_general(
                jnp.concatenate([spread[0], spread[1]], axis=1), rhs2[tile], NT, preferred_element_type=F32
            )
            if fresh:
                acc[...] = image
            else:
                acc[...] += image
        square = inner * inner
        return squares + square[:, 0:128] + square[:, 128:256]

    def document_sums():
        sums = []
        for group in range(4):
            side = pl.ds((group % 2) * 128, 128)
            tiles = [wbuf[(group // 2) * 4 + index, :, side] for index in range(4)]
            every = jnp.concatenate(tiles, axis=1)
            high = every.astype(BF16).astype(F32)
            both = jnp.concatenate([high, every - high], axis=0).astype(BF16)
            made = lax.dot_general(both, onehot[group], NT, preferred_element_type=F32)
            sums.append(made[0:8] + made[8:16])
        return sums

    def own_query(values):
        return jnp.sum(jnp.where(query_row == xy // 2, values, 0.0), axis=0, keepdims=True)

    message = pl.ds(0, 17)

    def send_all(copies):
        for copy in copies:
            copy.start()

    def sent_all(copies):
        for copy in copies:
            copy.wait_send()

    residual[...] = direction[...]
    norms = None
    scores = None
    for sweep in range(ITERS):
        last = sweep == ITERS - 1
        vector = direction[...]
        set_lhs(vector)
        squares = jnp.zeros((8, 128), F32)
        if sweep == 0:
            for place, (_, origin) in enumerate(near):
                squares = product(lax.rem(z + origin, 8), squares, place == 0, True)
            for index in range(4, 8):
                arrive(index)
                pass_on(index)
            sibling_tile(4, 5)
            prepare(lax.rem(z + 5, 8))
            sibling_tile(5, 3)
            prepare(lax.rem(z + 3, 8))
            sibling_tile(6, 4, upper)
            sibling_tile(7, 4, lower)
            prepare(lax.rem(z + 4, 8))
            for origin in (5, 3, 4):
                squares = product(lax.rem(z + origin, 8), squares, False, True)
        else:
            for tile in range(TILES):
                squares = product(tile, squares, tile == 0, not last)
        cube = vector.reshape(8, 32, 128)
        if not last:
            image = acc[:, 0:128] + acc[:, 128:256]
            usend[:, 0:16] = image.reshape(16, 16, 128)
            for index in range(16):
                usend[index, 16:17] = squares[index // 2 : index // 2 + 1]
            u_copies = [
                remote(usend.at[target, message], urecv.at[sweep, xy, message], u_send.at[sweep, index], u_recv.at[sweep, xy], device)
                for index, (target, device) in enumerate(plane)
            ]
            send_all(u_copies)
            urecv[sweep, xy, 0:17] = usend[xy, 0:17]
            if sweep == 0:
                for group in range(4):
                    for index in range(4):
                        chunk = ((group // 2) * 4 + index) * 2 + group % 2
                        onehot[group, :, index * 128 : (index + 1) * 128] = (doc_row == ft[chunk, 128:129]).astype(BF16)
            sums = document_sums()
            power = query_sum(cube * cube)
            if sweep == 0:
                norms = power
            for source, device in plane:
                remote(
                    usend.at[0, message], urecv.at[sweep, source, message], u_send.at[sweep, 0], u_recv.at[sweep, source], device
                ).wait_recv()
            total = jnp.sum(urecv[sweep, :, 0:17], axis=0)
            squared = jnp.sum(total[16:17], axis=1, keepdims=True)
            mine = own_query(norms) / (squared / tokens_all + DAMPING * own_query(power))
            own_image = total[0:16] / tokens_all + DAMPING * direction[own_rows, :]
            rbuf[sweep, xy, 0:16] = residual[own_rows, :] - mine * own_image
            rbuf[sweep, xy, 16:17] = jnp.broadcast_to(mine, (1, 128))
            r_copies = [
                remote(
                    rbuf.at[sweep, xy, message], rbuf.at[sweep, xy, message], r_send.at[sweep, index],
                    r_recv.at[sweep, xy], device,
                )
                for index, (_, device) in enumerate(plane)
            ]
            send_all(r_copies)
            pending.append(functools.partial(sent_all, r_copies))
            sent_all(u_copies)
            if sweep == 0:
                @pl.when(owns)
                def _():
                    sent_all(b_copies)

            for source, device in plane:
                remote(
                    rbuf.at[sweep, source, message], rbuf.at[sweep, source, message], r_send.at[sweep, 0],
                    r_recv.at[sweep, source], device,
                ).wait_recv()
            step_size = jnp.concatenate([rbuf[sweep, 2 * query, 16:17] for query in range(8)], axis=0)
            terms = [step_size * value for value in sums]
            scores = terms if scores is None else [a + b for a, b in zip(scores, terms)]
            left_over = rbuf[sweep, :, 0:16].reshape(256, 128)
            residual[...] = left_over
            cube_r = left_over.reshape(8, 32, 128)
            norms_next = query_sum(cube_r * cube_r)
            ratio = norms_next / norms
            direction[...] = (cube_r + ratio.reshape(8, 1, 1) * cube).reshape(256, 128)
            norms = norms_next

    ssend[...] = squares
    s_copies = [
        remote(ssend, srecv.at[xy], s_send.at[index], s_recv.at[xy], device)
        for index, (_, device) in enumerate(plane)
    ]
    send_all(s_copies)
    pending.append(functools.partial(sent_all, s_copies))
    srecv[xy] = squares
    power = query_sum(cube * cube)
    sums = document_sums()
    for source, device in plane:
        remote(ssend, srecv.at[source], s_send.at[0], s_recv.at[source], device).wait_recv()
    squared = jnp.sum(jnp.sum(srecv[...], axis=0), axis=1, keepdims=True)
    step_size = norms / (squared / tokens_all + DAMPING * power)

    for group in range(4):
        fsend[group] = (scores[group] + step_size * sums[group]) * (1.0 / 4096)

    def f_slot(where, height):
        return jnp.where(lax.rem(where, 2) == 0, height, 3 - height) * 4 + where

    own_slot = f_slot(low, zl)
    f_copies = [
        remote(fsend.at[where], frecv.at[own_slot], f_send.at[index], f_recv.at[own_slot], device)
        for index, (where, _, device) in enumerate(column)
    ]
    send_all(f_copies)
    pending.append(functools.partial(sent_all, f_copies))
    frecv[own_slot] = fsend[low]
    for copy in sent:
        copy.wait_send()
    for done in pending:
        done()
    for where, height, device in column:
        slot = f_slot(where, height)
        remote(fsend.at[0], frecv.at[slot], f_send.at[0], f_recv.at[slot], device).wait_recv()
    for where in range(16):
        diagonal, rest = where // 4, where % 4
        for row in range(4):
            begin = row * 32 + ((diagonal - row) % 4) * 8 + rest * 2
            order[begin : begin + 2] = frecv[where, 2 * row : 2 * row + 2]
    out[...] = order[...].T[0:16]


def local(inputs, out_grads, query_inputs, query_grads, in_proj, out_proj, doc_ids, query_ids):
    tokens_all = inputs.shape[0] * lax.axis_size("dp")
    hbm = pl.BlockSpec(memory_space=pltpu.HBM)
    vmem = pl.BlockSpec(memory_space=pltpu.VMEM)
    dma = pltpu.SemaphoreType.DMA
    return pl.pallas_call(
        functools.partial(kernel, float(tokens_all)),
        out_shape=jax.ShapeDtypeStruct((16, 128), F32),
        in_specs=[hbm] * 8,
        out_specs=vmem,
        scratch_shapes=[
            pltpu.VMEM((1, 512), jnp.int32),
            pltpu.VMEM((1, 128), jnp.int32),
            pltpu.VMEM((64, 1280), BF16),
            pltpu.VMEM((64, 6912), BF16),
            pltpu.VMEM((4, 128, 1280), BF16),
            pltpu.VMEM((4, 128, 6912), BF16),
            pltpu.VMEM((128, 1280), BF16),
            pltpu.VMEM((128, 6912), BF16),
            pltpu.VMEM((4, 128, 128), F32),
            pltpu.VMEM((128, 128), F32),
            pltpu.VMEM((4, 128, 128), F32),
            pltpu.VMEM((4, 128, 128), F32),
            pltpu.VMEM((16, 136, 128), F32),
            pltpu.VMEM((TILES, 256, 256), BF16),
            pltpu.VMEM((TILES, 256, 512), BF16),
            pltpu.VMEM((TILES, 64, 256), F32),
            pltpu.VMEM((512, 256), BF16),
            pltpu.VMEM((TILES, 8, 256), F32),
            pltpu.VMEM((256, 256), F32),
            pltpu.VMEM((4, 128, 512), BF16),
            pltpu.VMEM((256, 128), F32),
            pltpu.VMEM((256, 128), F32),
            pltpu.VMEM((16, 24, 128), F32),
            pltpu.VMEM((2, 16, 24, 128), F32),
            pltpu.VMEM((2, 16, 24, 128), F32),
            pltpu.VMEM((8, 128), F32),
            pltpu.VMEM((16, 8, 128), F32),
            pltpu.VMEM((4, 8, 128), F32),
            pltpu.VMEM((16, 8, 128), F32),
            pltpu.VMEM((128, 128), F32),
            dma((14,)),
            dma((4,)),
            dma((4,)),
            dma,
            dma((4,)),
            dma((8,)),
            dma((8,)),
            dma((9,)),
            dma((9,)),
            dma((16,)),
            dma((4,)),
            dma((2, 16)),
            dma((2, 16)),
            dma((2, 16)),
            dma((2, 16)),
            dma((16,)),
            dma((16,)),
            dma((16,)),
            dma((16,)),
        ],
        compiler_params=pltpu.CompilerParams(
            collective_id=0, has_side_effects=True, vmem_limit_bytes=62 * 1024 * 1024
        ),
    )(inputs, out_grads, query_inputs, query_grads, in_proj.T, out_proj.T, doc_ids, query_ids)


def solution(mesh):
    return jax.shard_map(
        local,
        mesh=mesh,
        in_specs=(
            P("dp", "tensor"),
            P("dp", "tensor"),
            P("dp", "tensor"),
            P("dp", "tensor"),
            P("tensor", None),
            P("tensor", None),
            P("dp", None),
            P("dp", None),
        ),
        out_specs=P("dp", None),
        check_vma=False,
    )
```

```python
import functools

import jax
import jax.numpy as jnp
from jax import lax
from jax.experimental import pallas as pl
from jax.experimental.pallas import tpu as pltpu
from jax.sharding import PartitionSpec as P

MESH = pl.DeviceIdType.MESH
F32, BF16 = jnp.float32, jnp.bfloat16
NT = (((1,), (1,)), ((), ()))
ITERS = 3
DAMPING = 0.1
TILES = 8


def split_bf16(value):
    high = value.astype(BF16)
    return high, (value - high.astype(F32)).astype(BF16)


def query_sum(value):
    return jnp.sum(jnp.sum(value, axis=1), axis=1, keepdims=True)


def kernel(
    tokens_all,
    inp, outg, qinp, qoutg, win, wout, ids_in, qids_in,
    out,
    ids, qids, win_v, wout_v, inp_v, outg_v, qinp_v, qoutg_v,
    part, qpart, rs, qrs, ft, rhs1, rhs2, feat_a, lhs, wbuf, acc, onehot,
    direction, residual, usend, urecv, rbuf, ssend, srecv, fsend, frecv, order,
    load_sem, rs_send, rs_recv, q_send, q_recv, ag_send, ag_recv, sib_send, sib_recv,
    b_send, b_recv, u_send, u_recv, r_send, r_recv, s_send, s_recv, f_send, f_recv,
):
    dp = lax.axis_index("dp")
    zl = lax.axis_index("tensor")
    low = lax.rem(dp, 4)
    core = lax.rem(dp, 2)
    half = low // 2
    xy = dp // 4
    xpos = lax.rem(xy, 4)
    ypos = xy // 4
    z = half * 4 + zl
    pending = []

    plane = [(lax.rem(xy + step, 16), (lax.rem(dp + 4 * step, 64), zl)) for step in range(1, 16)]
    lows = [low] + [lax.rem(low + step, 4) for step in range(1, 4)]
    zls = [zl] + [lax.rem(zl + step, 4) for step in range(1, 4)]
    column = [(lows[a], zls[b], (dp - low + lows[a], zls[b])) for a in range(4) for b in range(4) if a or b]

    barrier = pltpu.get_barrier_semaphore()
    for index in range(15):
        for device in (plane[index][1], column[index][2]):
            pl.semaphore_signal(barrier, inc=1, device_id=device, device_id_type=MESH)

    def up_column(offset, which=None):
        zpos = lax.rem(z + offset, 8)
        return (xy * 4 + (zpos // 4) * 2 + (core if which is None else which), lax.rem(zpos, 4))

    def remote(src, dst, send, recv, device):
        return pltpu.make_async_remote_copy(
            src_ref=src, dst_ref=dst, send_sem=send, recv_sem=recv, device_id=device, device_id_type=MESH
        )

    loads = [
        pltpu.make_async_copy(win, win_v, load_sem.at[0]),
        pltpu.make_async_copy(qinp, qinp_v, load_sem.at[1]),
        pltpu.make_async_copy(wout, wout_v, load_sem.at[2]),
        pltpu.make_async_copy(qoutg, qoutg_v, load_sem.at[3]),
        pltpu.make_async_copy(ids_in, ids, load_sem.at[12]),
        pltpu.make_async_copy(qids_in, qids, load_sem.at[13]),
    ]
    owners = [zls[2], zls[1], zls[3], zl]
    chunk_loads = []
    for step in range(4):
        rows = pl.ds(pl.multiple_of(owners[step] * 128, 128), 128)
        chunk_loads.append(
            (
                pltpu.make_async_copy(inp.at[rows, :], inp_v.at[step], load_sem.at[4 + step]),
                pltpu.make_async_copy(outg.at[rows, :], outg_v.at[step], load_sem.at[8 + step]),
            )
        )
    loads[0].start()
    loads[2].start()
    for pair in chunk_loads:
        for load in pair:
            load.start()
    for index in (1, 3, 4, 5):
        loads[index].start()

    def project(left, right):
        return jnp.concatenate(
            [
                lax.dot_general(win_v[...], left, NT, preferred_element_type=F32),
                lax.dot_general(wout_v[...], right, NT, preferred_element_type=F32),
            ],
            axis=0,
        )

    def project_chunk(step):
        for load in chunk_loads[step]:
            load.wait()
        part[step] = project(inp_v[step], outg_v[step])

    pieces = [pl.ds(0, 32), pl.ds(32, 32), pl.ds(64, 32), pl.ds(96, 32)]
    rs_copies = [
        [
            remote(
                part.at[step, pieces[piece]], rs.at[zl, pieces[piece]], rs_send.at[step, piece],
                rs_recv.at[zl, piece], (dp, owners[step]),
            )
            for piece in range(4)
        ]
        for step in range(3)
    ]
    diag = lax.rem(xpos + ypos, 4)
    query_owner = jnp.where(core == 0, diag, 3 - diag)
    owns = zl == query_owner
    q_copy = remote(qpart, qrs.at[zl], q_send, q_recv.at[zl], (dp, query_owner))

    loads[0].wait()
    loads[2].wait()
    project_chunk(0)
    project_chunk(1)
    pl.semaphore_wait(barrier, 30)
    for piece in range(4):
        rs_copies[0][piece].start()
        rs_copies[1][piece].start()
    project_chunk(2)
    for piece in range(4):
        rs_copies[2][piece].start()
    for index in (1, 3, 4, 5):
        loads[index].wait()
    qpart[...] = project(qinp_v[...], qoutg_v[...])

    @pl.when(jnp.logical_not(owns))
    def _():
        q_copy.start()

    project_chunk(3)
    rs[zl] = part[3]

    def first_done():
        @pl.when(jnp.logical_not(owns))
        def _():
            q_copy.wait_send()

        for copies in rs_copies:
            for copy in copies:
                copy.wait_send()

    pending.append(first_done)

    ids_own = jnp.zeros((1, 128), F32)
    for index in range(4):
        ids_own = ids_own + jnp.where(zl == index, ids[:, index * 128 : (index + 1) * 128].astype(F32), 0.0)
    own = z * 2 + core
    ft[own, 128:136] = jnp.broadcast_to(ids_own, (8, 128))

    whole = pl.ds(0, 129)
    pieces[3] = pl.ds(96, 33)
    halves = (pl.ds(0, 64), pl.ds(64, 65))
    sent = []

    def start(copy):
        copy.start()
        sent.append(copy)

    def handed(kind, piece, origin, target):
        where = ft.at[lax.rem(z + origin, 8) * 2 + core, pieces[piece], :]
        return remote(where, where, ag_send.at[kind, piece], ag_recv.at[kind, piece], up_column(target))

    def sibling(index, origin, rows, back=False):
        where = ft.at[lax.rem(z + origin, 8) * 2 + (1 - core if back else core), rows, :]
        return remote(where, where, sib_send.at[index], sib_recv.at[index], up_column(0, 1 - core))

    origins = (6, 2, 7, 1, 5, 3, 4, 4)

    def arrive(kind, piece):
        handed(kind, piece, origins[kind], 1).wait_recv()

    for piece in range(4):
        for step in range(1, 4):
            rows = pl.ds(piece * 32, 32)
            remote(
                part.at[0, rows], rs.at[zls[step], rows], rs_send.at[0, piece], rs_recv.at[zls[step], piece],
                (dp, zls[step]),
            ).wait_recv()
        span = slice(piece * 32, piece * 32 + 32)
        ft[own, span] = (rs[0, span] + rs[1, span]) + (rs[2, span] + rs[3, span])
        start(handed(0, piece, 0, 2))
        start(handed(1, piece, 0, 6))
    for piece in range(4):
        start(handed(2, piece, 0, 1))
        start(handed(3, piece, 0, 7))
    start(sibling(8, 0, whole))

    lane = lax.broadcasted_iota(jnp.int32, (128, 128), 1)
    pair_rows = pl.ds(pl.multiple_of(ypos * 64, 64), 64)
    b_copies = [
        remote(direction.at[pair_rows, :], direction.at[pair_rows, :], b_send.at[index], b_recv.at[ypos], device)
        for index, (_, device) in enumerate(plane)
    ]

    @pl.when(owns)
    def _():
        qrs[zl] = qpart[...]
        for step in range(1, 4):
            remote(qpart, qrs.at[zls[step]], q_send, q_recv.at[zls[step]], (dp, zls[step])).wait_recv()
        turned = (qrs[0] + qrs[1]) + (qrs[2] + qrs[3])
        feats = turned.T
        right = jnp.concatenate(
            [jnp.where(lane < 64, pltpu.roll(feats, 64, 1), 0.0), jnp.where(lane >= 64, feats, 0.0)], axis=0
        )
        rows = []
        for doc in range(2):
            mask = (qids[...] == doc).astype(F32)
            rows.append(jnp.concatenate([turned[0:32] * mask, turned[32:64] * mask], axis=1))
        direction[pair_rows, :] = jnp.dot(
            jnp.concatenate(rows, axis=0), right, precision=lax.Precision.HIGHEST, preferred_element_type=F32
        )
        for copy in b_copies:
            copy.start()

    for piece in range(4):
        arrive(0, piece)
        start(handed(4, piece, 6, 1))
        if piece < 2:
            start(handed(6, piece, 6, 2))
        arrive(1, piece)
        start(handed(5, piece, 2, 7))
        if piece >= 2:
            start(handed(7, piece, 2, 6))
    for kind in range(4):
        if kind >= 2:
            for piece in range(4):
                arrive(kind, piece)
        start(sibling(kind, origins[kind], whole))

    def prepare(tile):
        both = jnp.concatenate([ft[2 * tile], ft[2 * tile + 1]], axis=1)
        feat_a[tile] = both[0:64]
        high, rest = split_bf16(both[64:128])
        zero = jnp.zeros_like(high)
        rhs1[tile] = jnp.concatenate([high, high, rest, rest], axis=0)
        rhs2[tile] = jnp.concatenate(
            [
                jnp.concatenate([high, zero, rest, zero], axis=0),
                jnp.concatenate([zero, high, zero, rest], axis=0),
            ],
            axis=1,
        )

    near = [(8, 0), (0, 6), (1, 2), (2, 7), (3, 1)]
    for index, origin in near:
        sibling(index, origin, whole, True).wait_recv()
        prepare(lax.rem(z + origin, 8))
    far = [(4, 5, 0), (5, 3, 0), (6, 4, 0), (9, 5, 1), (10, 3, 1), (7, 4, 1)]
    for index, origin, side in far:
        kind = {5: 4, 3: 5, 4: 6 + side}[origin]
        for piece in (2 * side, 2 * side + 1):
            arrive(kind, piece)
        start(sibling(index, origin, halves[side]))

    for source in range(4):
        @pl.when(jnp.logical_not(jnp.logical_and(owns, ypos == source)))
        def _():
            rows = pl.ds(source * 64, 64)
            remote(
                direction.at[rows, :], direction.at[rows, :], b_send.at[0], b_recv.at[source], plane[0][1]
            ).wait_recv()

    lane_row = lax.broadcasted_iota(jnp.int32, (256, 128), 1)
    own_rows = pl.ds(pl.multiple_of(xy * 16, 16), 16)
    query_row = lax.broadcasted_iota(jnp.int32, (8, 1), 0)
    doc_row = lax.broadcasted_iota(jnp.int32, (128, 128), 0).astype(F32)

    def set_lhs(vector):
        high = vector.astype(BF16).astype(F32)
        rest = vector - high
        first = jnp.where(lane_row < 64, high, pltpu.roll(rest, 64, 1)).astype(BF16)
        second = jnp.where(lane_row < 64, pltpu.roll(high, 64, 1), rest).astype(BF16)
        lhs[0:256, 0:128] = first
        lhs[0:256, 128:256] = first
        lhs[256:512, 0:128] = second
        lhs[256:512, 128:256] = second

    def product(tile, squares, fresh, back):
        made = jnp.dot(lhs[...], rhs1[tile], preferred_element_type=F32)
        left = feat_a[tile].reshape(2, 1, 32, 256)
        inner = jnp.sum(jnp.sum(made.reshape(2, 8, 32, 256) * left, axis=0), axis=1)
        wbuf[tile] = inner
        if back:
            spread = (inner.reshape(1, 8, 1, 256) * left).reshape(2, 256, 256).astype(BF16)
            image = lax.dot_general(
                jnp.concatenate([spread[0], spread[1]], axis=1), rhs2[tile], NT, preferred_element_type=F32
            )
            if fresh:
                acc[...] = image
            else:
                acc[...] += image
        square = inner * inner
        return squares + square[:, 0:128] + square[:, 128:256]

    def document_sums():
        sums = []
        for group in range(4):
            side = pl.ds((group % 2) * 128, 128)
            tiles = [wbuf[(group // 2) * 4 + index, :, side] for index in range(4)]
            every = jnp.concatenate(tiles, axis=1)
            high = every.astype(BF16).astype(F32)
            both = jnp.concatenate([high, every - high], axis=0).astype(BF16)
            made = lax.dot_general(both, onehot[group], NT, preferred_element_type=F32)
            sums.append(made[0:8] + made[8:16])
        return sums

    def own_query(values):
        return jnp.sum(jnp.where(query_row == xy // 2, values, 0.0), axis=0, keepdims=True)

    message = pl.ds(0, 17)

    def send_all(copies):
        for copy in copies:
            copy.start()

    def sent_all(copies):
        for copy in copies:
            copy.wait_send()

    residual[...] = direction[...]
    norms = None
    scores = None
    for sweep in range(ITERS):
        last = sweep == ITERS - 1
        vector = direction[...]
        set_lhs(vector)
        squares = jnp.zeros((8, 128), F32)
        if sweep == 0:
            for place, (_, origin) in enumerate(near):
                squares = product(lax.rem(z + origin, 8), squares, place == 0, True)
            for index, origin, side in far:
                sibling(index, origin, halves[side], True).wait_recv()
            for origin in (5, 3, 4):
                prepare(lax.rem(z + origin, 8))
            for origin in (5, 3, 4):
                squares = product(lax.rem(z + origin, 8), squares, False, True)
        else:
            for tile in range(TILES):
                squares = product(tile, squares, tile == 0, not last)
        cube = vector.reshape(8, 32, 128)
        if not last:
            image = acc[:, 0:128] + acc[:, 128:256]
            usend[:, 0:16] = image.reshape(16, 16, 128)
            for index in range(16):
                usend[index, 16:17] = squares[index // 2 : index // 2 + 1]
            u_copies = [
                remote(usend.at[target, message], urecv.at[sweep, xy, message], u_send.at[sweep, index], u_recv.at[sweep, xy], device)
                for index, (target, device) in enumerate(plane)
            ]
            send_all(u_copies)
            urecv[sweep, xy, 0:17] = usend[xy, 0:17]
            if sweep == 0:
                for group in range(4):
                    for index in range(4):
                        chunk = ((group // 2) * 4 + index) * 2 + group % 2
                        onehot[group, :, index * 128 : (index + 1) * 128] = (doc_row == ft[chunk, 128:129]).astype(BF16)
            sums = document_sums()
            power = query_sum(cube * cube)
            if sweep == 0:
                norms = power
            for source, device in plane:
                remote(
                    usend.at[0, message], urecv.at[sweep, source, message], u_send.at[sweep, 0], u_recv.at[sweep, source], device
                ).wait_recv()
            total = jnp.sum(urecv[sweep, :, 0:17], axis=0)
            squared = jnp.sum(total[16:17], axis=1, keepdims=True)
            mine = own_query(norms) / (squared / tokens_all + DAMPING * own_query(power))
            own_image = total[0:16] / tokens_all + DAMPING * direction[own_rows, :]
            rbuf[sweep, xy, 0:16] = residual[own_rows, :] - mine * own_image
            rbuf[sweep, xy, 16:17] = jnp.broadcast_to(mine, (1, 128))
            r_copies = [
                remote(
                    rbuf.at[sweep, xy, message], rbuf.at[sweep, xy, message], r_send.at[sweep, index],
                    r_recv.at[sweep, xy], device,
                )
                for index, (_, device) in enumerate(plane)
            ]
            send_all(r_copies)
            pending.append(functools.partial(sent_all, r_copies))
            sent_all(u_copies)
            if sweep == 0:
                @pl.when(owns)
                def _():
                    sent_all(b_copies)

            for source, device in plane:
                remote(
                    rbuf.at[sweep, source, message], rbuf.at[sweep, source, message], r_send.at[sweep, 0],
                    r_recv.at[sweep, source], device,
                ).wait_recv()
            step_size = jnp.concatenate([rbuf[sweep, 2 * query, 16:17] for query in range(8)], axis=0)
            terms = [step_size * value for value in sums]
            scores = terms if scores is None else [a + b for a, b in zip(scores, terms)]
            left_over = rbuf[sweep, :, 0:16].reshape(256, 128)
            residual[...] = left_over
            cube_r = left_over.reshape(8, 32, 128)
            norms_next = query_sum(cube_r * cube_r)
            ratio = norms_next / norms
            direction[...] = (cube_r + ratio.reshape(8, 1, 1) * cube).reshape(256, 128)
            norms = norms_next

    ssend[...] = squares
    s_copies = [
        remote(ssend, srecv.at[xy], s_send.at[index], s_recv.at[xy], device)
        for index, (_, device) in enumerate(plane)
    ]
    send_all(s_copies)
    pending.append(functools.partial(sent_all, s_copies))
    srecv[xy] = squares
    power = query_sum(cube * cube)
    sums = document_sums()
    for source, device in plane:
        remote(ssend, srecv.at[source], s_send.at[0], s_recv.at[source], device).wait_recv()
    squared = jnp.sum(jnp.sum(srecv[...], axis=0), axis=1, keepdims=True)
    step_size = norms / (squared / tokens_all + DAMPING * power)

    for group in range(4):
        fsend[group] = (scores[group] + step_size * sums[group]) * (1.0 / 4096)

    def f_slot(where, height):
        return jnp.where(lax.rem(where, 2) == 0, height, 3 - height) * 4 + where

    own_slot = f_slot(low, zl)
    f_copies = [
        remote(fsend.at[where], frecv.at[own_slot], f_send.at[index], f_recv.at[own_slot], device)
        for index, (where, _, device) in enumerate(column)
    ]
    send_all(f_copies)
    pending.append(functools.partial(sent_all, f_copies))
    frecv[own_slot] = fsend[low]
    for copy in sent:
        copy.wait_send()
    for done in pending:
        done()
    for where, height, device in column:
        slot = f_slot(where, height)
        remote(fsend.at[0], frecv.at[slot], f_send.at[0], f_recv.at[slot], device).wait_recv()
    for where in range(16):
        diagonal, rest = where // 4, where % 4
        for row in range(4):
            begin = row * 32 + ((diagonal - row) % 4) * 8 + rest * 2
            order[begin : begin + 2] = frecv[where, 2 * row : 2 * row + 2]
    out[...] = order[...].T[0:16]


def local(inputs, out_grads, query_inputs, query_grads, in_proj, out_proj, doc_ids, query_ids):
    tokens_all = inputs.shape[0] * lax.axis_size("dp")
    hbm = pl.BlockSpec(memory_space=pltpu.HBM)
    vmem = pl.BlockSpec(memory_space=pltpu.VMEM)
    dma = pltpu.SemaphoreType.DMA
    return pl.pallas_call(
        functools.partial(kernel, float(tokens_all)),
        out_shape=jax.ShapeDtypeStruct((16, 128), F32),
        in_specs=[hbm] * 8,
        out_specs=vmem,
        scratch_shapes=[
            pltpu.VMEM((1, 512), jnp.int32),
            pltpu.VMEM((1, 128), jnp.int32),
            pltpu.VMEM((64, 1280), BF16),
            pltpu.VMEM((64, 6912), BF16),
            pltpu.VMEM((4, 128, 1280), BF16),
            pltpu.VMEM((4, 128, 6912), BF16),
            pltpu.VMEM((128, 1280), BF16),
            pltpu.VMEM((128, 6912), BF16),
            pltpu.VMEM((4, 128, 128), F32),
            pltpu.VMEM((128, 128), F32),
            pltpu.VMEM((4, 128, 128), F32),
            pltpu.VMEM((4, 128, 128), F32),
            pltpu.VMEM((16, 136, 128), F32),
            pltpu.VMEM((TILES, 256, 256), BF16),
            pltpu.VMEM((TILES, 256, 512), BF16),
            pltpu.VMEM((TILES, 64, 256), F32),
            pltpu.VMEM((512, 256), BF16),
            pltpu.VMEM((TILES, 8, 256), F32),
            pltpu.VMEM((256, 256), F32),
            pltpu.VMEM((4, 128, 512), BF16),
            pltpu.VMEM((256, 128), F32),
            pltpu.VMEM((256, 128), F32),
            pltpu.VMEM((16, 24, 128), F32),
            pltpu.VMEM((2, 16, 24, 128), F32),
            pltpu.VMEM((2, 16, 24, 128), F32),
            pltpu.VMEM((8, 128), F32),
            pltpu.VMEM((16, 8, 128), F32),
            pltpu.VMEM((4, 8, 128), F32),
            pltpu.VMEM((16, 8, 128), F32),
            pltpu.VMEM((128, 128), F32),
            dma((14,)),
            dma((3, 4)),
            dma((4, 4)),
            dma,
            dma((4,)),
            dma((8, 4)),
            dma((8, 4)),
            dma((11,)),
            dma((11,)),
            dma((16,)),
            dma((4,)),
            dma((2, 16)),
            dma((2, 16)),
            dma((2, 16)),
            dma((2, 16)),
            dma((16,)),
            dma((16,)),
            dma((16,)),
            dma((16,)),
        ],
        compiler_params=pltpu.CompilerParams(
            collective_id=0, has_side_effects=True, vmem_limit_bytes=62 * 1024 * 1024
        ),
    )(inputs, out_grads, query_inputs, query_grads, in_proj.T, out_proj.T, doc_ids, query_ids)


def solution(mesh):
    return jax.shard_map(
        local,
        mesh=mesh,
        in_specs=(
            P("dp", "tensor"),
            P("dp", "tensor"),
            P("dp", "tensor"),
            P("dp", "tensor"),
            P("tensor", None),
            P("tensor", None),
            P("dp", None),
            P("dp", None),
        ),
        out_specs=P("dp", None),
        check_vma=False,
    )
```

```python
import functools

import jax
import jax.numpy as jnp
from jax import lax
from jax.experimental import pallas as pl
from jax.experimental.pallas import tpu as pltpu
from jax.sharding import PartitionSpec as P

MESH = pl.DeviceIdType.MESH
F32, BF16 = jnp.float32, jnp.bfloat16
NT = (((1,), (1,)), ((), ()))
ITERS = 3
DAMPING = 0.1
TILES = 8


def split_bf16(value):
    high = value.astype(BF16)
    return high, (value - high.astype(F32)).astype(BF16)


def query_sum(value):
    return jnp.sum(jnp.sum(value, axis=1), axis=1, keepdims=True)


def kernel(
    tokens_all,
    inp, outg, qinp, qoutg, win, wout, ids_in, qids_in,
    out,
    ids, qids, win_v, wout_v, inp_v, outg_v, qinp_v, qoutg_v,
    part, qpart, rs, qrs, ft, rhs1, rhs2, feat_a, lhs, wbuf, acc, onehot,
    direction, residual, usend, urecv, rbuf, ssend, srecv, fsend, frecv, order, lined,
    load_sem, rs_send, rs_recv, q_send, q_recv, ag_send, ag_recv, sib_send, sib_recv,
    b_send, b_recv, u_send, u_recv, r_send, r_recv, s_send, s_recv, f_send, f_recv,
):
    dp = lax.axis_index("dp")
    zl = lax.axis_index("tensor")
    low = lax.rem(dp, 4)
    core = lax.rem(dp, 2)
    half = low // 2
    xy = dp // 4
    xpos = lax.rem(xy, 4)
    ypos = xy // 4
    z = half * 4 + zl
    pending = []

    plane = [(lax.rem(xy + step, 16), (lax.rem(dp + 4 * step, 64), zl)) for step in range(1, 16)]
    lows = [low] + [lax.rem(low + step, 4) for step in range(1, 4)]
    zls = [zl] + [lax.rem(zl + step, 4) for step in range(1, 4)]
    column = [(lows[a], zls[b], (dp - low + lows[a], zls[b])) for a in range(4) for b in range(4) if a or b]

    barrier = pltpu.get_barrier_semaphore()
    for index in range(15):
        for device in (plane[index][1], column[index][2]):
            pl.semaphore_signal(barrier, inc=1, device_id=device, device_id_type=MESH)

    def up_column(offset, which=None):
        zpos = lax.rem(z + offset, 8)
        return (xy * 4 + (zpos // 4) * 2 + (core if which is None else which), lax.rem(zpos, 4))

    def remote(src, dst, send, recv, device):
        return pltpu.make_async_remote_copy(
            src_ref=src, dst_ref=dst, send_sem=send, recv_sem=recv, device_id=device, device_id_type=MESH
        )

    loads = [
        pltpu.make_async_copy(win, win_v, load_sem.at[0]),
        pltpu.make_async_copy(qinp, qinp_v, load_sem.at[1]),
        pltpu.make_async_copy(wout, wout_v, load_sem.at[2]),
        pltpu.make_async_copy(qoutg, qoutg_v, load_sem.at[3]),
        pltpu.make_async_copy(ids_in, ids, load_sem.at[12]),
        pltpu.make_async_copy(qids_in, qids, load_sem.at[13]),
    ]
    owners = [zls[2], zls[1], zls[3], zl]
    chunk_loads = []
    for step in range(4):
        rows = pl.ds(pl.multiple_of(owners[step] * 128, 128), 128)
        chunk_loads.append(
            (
                pltpu.make_async_copy(inp.at[rows, :], inp_v.at[step], load_sem.at[4 + step]),
                pltpu.make_async_copy(outg.at[rows, :], outg_v.at[step], load_sem.at[8 + step]),
            )
        )
    def begin(some):
        for load in some:
            load.start()

    begin((loads[0], loads[2]))
    begin(chunk_loads[0])
    begin((loads[1], loads[3], loads[4], loads[5]))

    def project(left, right):
        return jnp.concatenate(
            [
                lax.dot_general(win_v[...], left, NT, preferred_element_type=F32),
                lax.dot_general(wout_v[...], right, NT, preferred_element_type=F32),
            ],
            axis=0,
        )

    def project_chunk(step):
        for load in chunk_loads[step]:
            load.wait()
        part[step] = project(inp_v[step], outg_v[step])

    pieces = [pl.ds(0, 32), pl.ds(32, 32), pl.ds(64, 32), pl.ds(96, 32)]
    rs_copies = [
        [
            remote(
                part.at[step, pieces[piece]], rs.at[zl, pieces[piece]], rs_send.at[step, piece],
                rs_recv.at[zl, piece], (dp, owners[step]),
            )
            for piece in range(4)
        ]
        for step in range(3)
    ]
    diag = lax.rem(xpos + ypos, 4)
    query_owner = jnp.where(core == 0, diag, 3 - diag)
    owns = zl == query_owner
    q_copy = remote(qpart, qrs.at[zl], q_send, q_recv.at[zl], (dp, query_owner))

    loads[0].wait()
    loads[2].wait()
    project_chunk(0)
    begin(chunk_loads[1])
    begin(chunk_loads[2])
    for index in (1, 3, 4, 5):
        loads[index].wait()
    qpart[...] = project(qinp_v[...], qoutg_v[...])
    begin(chunk_loads[3])
    pl.semaphore_wait(barrier, 30)
    for copy in rs_copies[0]:
        copy.start()

    @pl.when(jnp.logical_not(owns))
    def _():
        q_copy.start()

    for step in (1, 2):
        project_chunk(step)
        for copy in rs_copies[step]:
            copy.start()
    project_chunk(3)
    rs[zl] = part[3]

    def first_done():
        @pl.when(jnp.logical_not(owns))
        def _():
            q_copy.wait_send()

        for copies in rs_copies:
            for copy in copies:
                copy.wait_send()

    pending.append(first_done)

    lane = lax.broadcasted_iota(jnp.int32, (128, 128), 1)
    pair_rows = pl.ds(pl.multiple_of(ypos * 64, 64), 64)
    b_copies = [
        remote(direction.at[pair_rows, :], direction.at[pair_rows, :], b_send.at[index], b_recv.at[ypos], device)
        for index, (_, device) in enumerate(plane)
    ]

    @pl.when(owns)
    def _():
        qrs[zl] = qpart[...]
        for step in range(1, 4):
            remote(qpart, qrs.at[zls[step]], q_send, q_recv.at[zls[step]], (dp, zls[step])).wait_recv()
        turned = (qrs[0] + qrs[1]) + (qrs[2] + qrs[3])
        feats = turned.T
        right = jnp.concatenate(
            [jnp.where(lane < 64, pltpu.roll(feats, 64, 1), 0.0), jnp.where(lane >= 64, feats, 0.0)], axis=0
        )
        rows = []
        for doc in range(2):
            mask = (qids[...] == doc).astype(F32)
            rows.append(jnp.concatenate([turned[0:32] * mask, turned[32:64] * mask], axis=1))
        direction[pair_rows, :] = jnp.dot(
            jnp.concatenate(rows, axis=0), right, precision=lax.Precision.HIGHEST, preferred_element_type=F32
        )
        for copy in b_copies:
            copy.start()

    ids_own = jnp.zeros((1, 128), F32)
    for index in range(4):
        ids_own = ids_own + jnp.where(zl == index, ids[:, index * 128 : (index + 1) * 128].astype(F32), 0.0)
    own = z * 2 + core
    ft[own, 128:136] = jnp.broadcast_to(ids_own, (8, 128))

    whole = pl.ds(0, 129)
    pieces[3] = pl.ds(96, 33)
    halves = (pl.ds(0, 64), pl.ds(64, 65))
    sent = []

    def start(copy):
        copy.start()
        sent.append(copy)

    def handed(kind, piece, origin, target):
        where = ft.at[lax.rem(z + origin, 8) * 2 + core, pieces[piece], :]
        return remote(where, where, ag_send.at[kind, piece], ag_recv.at[kind, piece], up_column(target))

    def sibling(index, origin, rows, back=False):
        where = ft.at[lax.rem(z + origin, 8) * 2 + (1 - core if back else core), rows, :]
        return remote(where, where, sib_send.at[index], sib_recv.at[index], up_column(0, 1 - core))

    origins = (6, 2, 7, 1, 5, 3, 4, 4)

    def arrive(kind, piece):
        handed(kind, piece, origins[kind], 1).wait_recv()

    for piece in range(4):
        for step in range(1, 4):
            rows = pl.ds(piece * 32, 32)
            remote(
                part.at[0, rows], rs.at[zls[step], rows], rs_send.at[0, piece], rs_recv.at[zls[step], piece],
                (dp, zls[step]),
            ).wait_recv()
        span = slice(piece * 32, piece * 32 + 32)
        ft[own, span] = (rs[0, span] + rs[1, span]) + (rs[2, span] + rs[3, span])
        start(handed(0, piece, 0, 2))
        start(handed(1, piece, 0, 6))
    for piece in range(4):
        start(handed(2, piece, 0, 1))
        start(handed(3, piece, 0, 7))
    start(sibling(8, 0, whole))

    for piece in range(4):
        arrive(0, piece)
        start(handed(4, piece, 6, 1))
        if piece < 2:
            start(handed(6, piece, 6, 2))
        arrive(1, piece)
        start(handed(5, piece, 2, 7))
        if piece >= 2:
            start(handed(7, piece, 2, 6))
    for kind in range(4):
        if kind >= 2:
            for piece in range(4):
                arrive(kind, piece)
        start(sibling(kind, origins[kind], whole))

    def prepare(tile):
        both = jnp.concatenate([ft[2 * tile], ft[2 * tile + 1]], axis=1)
        feat_a[tile] = both[0:64]
        high, rest = split_bf16(both[64:128])
        zero = jnp.zeros_like(high)
        rhs1[tile] = jnp.concatenate([high, high, rest, rest], axis=0)
        rhs2[tile] = jnp.concatenate(
            [
                jnp.concatenate([high, zero, rest, zero], axis=0),
                jnp.concatenate([zero, high, zero, rest], axis=0),
            ],
            axis=1,
        )

    near = [(8, 0), (0, 6), (1, 2), (2, 7), (3, 1)]
    for index, origin in near:
        sibling(index, origin, whole, True).wait_recv()
        prepare(lax.rem(z + origin, 8))
    far = [(4, 5, 0), (5, 3, 0), (6, 4, 0), (9, 5, 1), (10, 3, 1), (7, 4, 1)]
    for index, origin, side in far:
        kind = {5: 4, 3: 5, 4: 6 + side}[origin]
        for piece in (2 * side, 2 * side + 1):
            arrive(kind, piece)
        start(sibling(index, origin, halves[side]))

    for source in range(4):
        @pl.when(jnp.logical_not(jnp.logical_and(owns, ypos == source)))
        def _():
            rows = pl.ds(source * 64, 64)
            remote(
                direction.at[rows, :], direction.at[rows, :], b_send.at[0], b_recv.at[source], plane[0][1]
            ).wait_recv()

    lane_row = lax.broadcasted_iota(jnp.int32, (256, 128), 1)
    own_rows = pl.ds(pl.multiple_of(xy * 16, 16), 16)
    query_row = lax.broadcasted_iota(jnp.int32, (8, 1), 0)
    doc_row = lax.broadcasted_iota(jnp.int32, (128, 128), 0).astype(F32)

    def set_lhs(vector):
        high = vector.astype(BF16).astype(F32)
        rest = vector - high
        first = jnp.where(lane_row < 64, high, pltpu.roll(rest, 64, 1)).astype(BF16)
        second = jnp.where(lane_row < 64, pltpu.roll(high, 64, 1), rest).astype(BF16)
        lhs[0:256, 0:128] = first
        lhs[0:256, 128:256] = first
        lhs[256:512, 0:128] = second
        lhs[256:512, 128:256] = second

    def product(tile, squares, fresh, back):
        made = jnp.dot(lhs[...], rhs1[tile], preferred_element_type=F32)
        left = feat_a[tile].reshape(2, 1, 32, 256)
        inner = jnp.sum(jnp.sum(made.reshape(2, 8, 32, 256) * left, axis=0), axis=1)
        wbuf[tile] = inner
        if back:
            spread = (inner.reshape(1, 8, 1, 256) * left).reshape(2, 256, 256).astype(BF16)
            image = lax.dot_general(
                jnp.concatenate([spread[0], spread[1]], axis=1), rhs2[tile], NT, preferred_element_type=F32
            )
            if fresh:
                acc[...] = image
            else:
                acc[...] += image
        square = inner * inner
        return squares + square[:, 0:128] + square[:, 128:256]

    def document_sums():
        sums = []
        for group in range(4):
            side = pl.ds((group % 2) * 128, 128)
            tiles = [wbuf[(group // 2) * 4 + index, :, side] for index in range(4)]
            every = jnp.concatenate(tiles, axis=1)
            high = every.astype(BF16).astype(F32)
            both = jnp.concatenate([high, every - high], axis=0).astype(BF16)
            made = lax.dot_general(both, onehot[group], NT, preferred_element_type=F32)
            sums.append(made[0:8] + made[8:16])
        return sums

    def own_query(values):
        return jnp.sum(jnp.where(query_row == xy // 2, values, 0.0), axis=0, keepdims=True)

    message = pl.ds(0, 17)

    def send_all(copies):
        for copy in copies:
            copy.start()

    def sent_all(copies):
        for copy in copies:
            copy.wait_send()

    residual[...] = direction[...]
    norms = None
    scores = None
    for sweep in range(ITERS):
        last = sweep == ITERS - 1
        vector = direction[...]
        set_lhs(vector)
        squares = jnp.zeros((8, 128), F32)
        if sweep == 0:
            for place, (_, origin) in enumerate(near):
                squares = product(lax.rem(z + origin, 8), squares, place == 0, True)
            for index, origin, side in far:
                sibling(index, origin, halves[side], True).wait_recv()
            for origin in (5, 3, 4):
                prepare(lax.rem(z + origin, 8))
            for origin in (5, 3, 4):
                squares = product(lax.rem(z + origin, 8), squares, False, True)
        else:
            for tile in range(TILES):
                squares = product(tile, squares, tile == 0, not last)
        cube = vector.reshape(8, 32, 128)
        if not last:
            image = acc[:, 0:128] + acc[:, 128:256]
            usend[:, 0:16] = image.reshape(16, 16, 128)
            for index in range(16):
                usend[index, 16:17] = squares[index // 2 : index // 2 + 1]
            u_copies = [
                remote(usend.at[target, message], urecv.at[sweep, xy, message], u_send.at[sweep, index], u_recv.at[sweep, xy], device)
                for index, (target, device) in enumerate(plane)
            ]
            send_all(u_copies)
            urecv[sweep, xy, 0:17] = usend[xy, 0:17]
            if sweep == 0:
                for group in range(4):
                    for index in range(4):
                        chunk = ((group // 2) * 4 + index) * 2 + group % 2
                        onehot[group, :, index * 128 : (index + 1) * 128] = (doc_row == ft[chunk, 128:129]).astype(BF16)
            sums = document_sums()
            power = query_sum(cube * cube)
            if sweep == 0:
                norms = power
            for source, device in plane:
                remote(
                    usend.at[0, message], urecv.at[sweep, source, message], u_send.at[sweep, 0], u_recv.at[sweep, source], device
                ).wait_recv()
            total = jnp.sum(urecv[sweep, :, 0:17], axis=0)
            squared = jnp.sum(total[16:17], axis=1, keepdims=True)
            mine = own_query(norms) / (squared / tokens_all + DAMPING * own_query(power))
            own_image = total[0:16] / tokens_all + DAMPING * direction[own_rows, :]
            rbuf[sweep, xy, 0:16] = residual[own_rows, :] - mine * own_image
            rbuf[sweep, xy, 16:17] = jnp.broadcast_to(mine, (1, 128))
            r_copies = [
                remote(
                    rbuf.at[sweep, xy, message], rbuf.at[sweep, xy, message], r_send.at[sweep, index],
                    r_recv.at[sweep, xy], device,
                )
                for index, (_, device) in enumerate(plane)
            ]
            send_all(r_copies)
            pending.append(functools.partial(sent_all, r_copies))
            sent_all(u_copies)
            if sweep == 0:
                @pl.when(owns)
                def _():
                    sent_all(b_copies)

            for source, device in plane:
                remote(
                    rbuf.at[sweep, source, message], rbuf.at[sweep, source, message], r_send.at[sweep, 0],
                    r_recv.at[sweep, source], device,
                ).wait_recv()
            step_size = jnp.concatenate([rbuf[sweep, 2 * query, 16:17] for query in range(8)], axis=0)
            terms = [step_size * value for value in sums]
            scores = terms if scores is None else [a + b for a, b in zip(scores, terms)]
            left_over = rbuf[sweep, :, 0:16].reshape(256, 128)
            residual[...] = left_over
            cube_r = left_over.reshape(8, 32, 128)
            norms_next = query_sum(cube_r * cube_r)
            ratio = norms_next / norms
            direction[...] = (cube_r + ratio.reshape(8, 1, 1) * cube).reshape(256, 128)
            norms = norms_next

    ssend[...] = squares
    s_copies = [
        remote(ssend, srecv.at[xy], s_send.at[index], s_recv.at[xy], device)
        for index, (_, device) in enumerate(plane)
    ]
    send_all(s_copies)
    pending.append(functools.partial(sent_all, s_copies))
    srecv[xy] = squares
    power = query_sum(cube * cube)
    sums = document_sums()
    for source, device in plane:
        remote(ssend, srecv.at[source], s_send.at[0], s_recv.at[source], device).wait_recv()
    squared = jnp.sum(jnp.sum(srecv[...], axis=0), axis=1, keepdims=True)
    step_size = norms / (squared / tokens_all + DAMPING * power)

    for group in range(4):
        made = jnp.where(lane[0:8] < 16, (scores[group] + step_size * sums[group]) * (1.0 / 4096), 0.0)
        turned = [made[0:1]] + [pltpu.roll(made[query : query + 1], 16 * query, 1) for query in range(1, 8)]
        row = (turned[0] + turned[1]) + (turned[2] + turned[3]) + ((turned[4] + turned[5]) + (turned[6] + turned[7]))
        fsend[group, 0:1] = row

    def f_slot(where, height):
        return jnp.where(lax.rem(where, 2) == 0, height, 3 - height) * 4 + where

    own_slot = f_slot(low, zl)
    one_row = pl.ds(0, 1)
    f_copies = [
        remote(fsend.at[where, one_row], frecv.at[own_slot, one_row], f_send.at[index], f_recv.at[own_slot], device)
        for index, (where, _, device) in enumerate(column)
    ]
    send_all(f_copies)
    pending.append(functools.partial(sent_all, f_copies))
    frecv[own_slot, 0:1] = fsend[low, 0:1]
    for copy in sent:
        copy.wait_send()
    for done in pending:
        done()
    for where, height, device in column:
        slot = f_slot(where, height)
        remote(fsend.at[0, one_row], frecv.at[slot, one_row], f_send.at[0], f_recv.at[slot], device).wait_recv()
    for where in range(16):
        lined[where : where + 1] = frecv[where, 0:1]
    for query in range(8):
        row, which = query // 2, query % 2
        places = lined[...] if query == 0 else pltpu.roll(lined[...], 128 - 16 * query, 1)
        for diagonal in range(4):
            begin_row = row * 32 + ((diagonal - row) % 4) * 8 + which
            order[pl.ds(begin_row, 4, stride=2)] = places[4 * diagonal : 4 * diagonal + 4]
    out[...] = order[...].T[0:16]


def local(inputs, out_grads, query_inputs, query_grads, in_proj, out_proj, doc_ids, query_ids):
    tokens_all = inputs.shape[0] * lax.axis_size("dp")
    hbm = pl.BlockSpec(memory_space=pltpu.HBM)
    vmem = pl.BlockSpec(memory_space=pltpu.VMEM)
    dma = pltpu.SemaphoreType.DMA
    return pl.pallas_call(
        functools.partial(kernel, float(tokens_all)),
        out_shape=jax.ShapeDtypeStruct((16, 128), F32),
        in_specs=[hbm] * 8,
        out_specs=vmem,
        scratch_shapes=[
            pltpu.VMEM((1, 512), jnp.int32),
            pltpu.VMEM((1, 128), jnp.int32),
            pltpu.VMEM((64, 1280), BF16),
            pltpu.VMEM((64, 6912), BF16),
            pltpu.VMEM((4, 128, 1280), BF16),
            pltpu.VMEM((4, 128, 6912), BF16),
            pltpu.VMEM((128, 1280), BF16),
            pltpu.VMEM((128, 6912), BF16),
            pltpu.VMEM((4, 128, 128), F32),
            pltpu.VMEM((128, 128), F32),
            pltpu.VMEM((4, 128, 128), F32),
            pltpu.VMEM((4, 128, 128), F32),
            pltpu.VMEM((16, 136, 128), F32),
            pltpu.VMEM((TILES, 256, 256), BF16),
            pltpu.VMEM((TILES, 256, 512), BF16),
            pltpu.VMEM((TILES, 64, 256), F32),
            pltpu.VMEM((512, 256), BF16),
            pltpu.VMEM((TILES, 8, 256), F32),
            pltpu.VMEM((256, 256), F32),
            pltpu.VMEM((4, 128, 512), BF16),
            pltpu.VMEM((256, 128), F32),
            pltpu.VMEM((256, 128), F32),
            pltpu.VMEM((16, 24, 128), F32),
            pltpu.VMEM((2, 16, 24, 128), F32),
            pltpu.VMEM((2, 16, 24, 128), F32),
            pltpu.VMEM((8, 128), F32),
            pltpu.VMEM((16, 8, 128), F32),
            pltpu.VMEM((4, 8, 128), F32),
            pltpu.VMEM((16, 8, 128), F32),
            pltpu.VMEM((128, 128), F32),
            pltpu.VMEM((16, 128), F32),
            dma((14,)),
            dma((3, 4)),
            dma((4, 4)),
            dma,
            dma((4,)),
            dma((8, 4)),
            dma((8, 4)),
            dma((11,)),
            dma((11,)),
            dma((16,)),
            dma((4,)),
            dma((2, 16)),
            dma((2, 16)),
            dma((2, 16)),
            dma((2, 16)),
            dma((16,)),
            dma((16,)),
            dma((16,)),
            dma((16,)),
        ],
        compiler_params=pltpu.CompilerParams(
            collective_id=0, has_side_effects=True, vmem_limit_bytes=62 * 1024 * 1024
        ),
    )(inputs, out_grads, query_inputs, query_grads, in_proj.T, out_proj.T, doc_ids, query_ids)


def solution(mesh):
    return jax.shard_map(
        local,
        mesh=mesh,
        in_specs=(
            P("dp", "tensor"),
            P("dp", "tensor"),
            P("dp", "tensor"),
            P("dp", "tensor"),
            P("tensor", None),
            P("tensor", None),
            P("dp", None),
            P("dp", None),
        ),
        out_specs=P("dp", None),
        check_vma=False,
    )
```

```python
import functools

import jax
import jax.numpy as jnp
from jax import lax
from jax.experimental import pallas as pl
from jax.experimental.pallas import tpu as pltpu
from jax.sharding import PartitionSpec as P

MESH = pl.DeviceIdType.MESH
F32, BF16 = jnp.float32, jnp.bfloat16
NT = (((1,), (1,)), ((), ()))
ITERS = 3
DAMPING = 0.1
TILES = 8


def split_bf16(value):
    high = value.astype(BF16)
    return high, (value - high.astype(F32)).astype(BF16)


def query_sum(value):
    return jnp.sum(jnp.sum(value, axis=1), axis=1, keepdims=True)


def kernel(
    tokens_all,
    inp, outg, qinp, qoutg, win, wout, ids_in, qids_in,
    out,
    ids, qids, win_v, wout_v, inp_v, outg_v, qinp_v, qoutg_v,
    part, qpart, rs, qrs, ft, rhs1, rhs2, feat_a, lhs, wbuf, acc, onehot,
    direction, residual, usend, urecv, rbuf, ssend, srecv, fsend, frecv, order, lined,
    load_sem, rs_send, rs_recv, q_send, q_recv, ag_send, ag_recv, sib_send, sib_recv,
    b_send, b_recv, u_send, u_recv, r_send, r_recv, s_send, s_recv, f_send, f_recv,
):
    dp = lax.axis_index("dp")
    zl = lax.axis_index("tensor")
    low = lax.rem(dp, 4)
    core = lax.rem(dp, 2)
    half = low // 2
    xy = dp // 4
    xpos = lax.rem(xy, 4)
    ypos = xy // 4
    z = half * 4 + zl
    pending = []

    plane = [(lax.rem(xy + step, 16), (lax.rem(dp + 4 * step, 64), zl)) for step in range(1, 16)]
    lows = [low] + [lax.rem(low + step, 4) for step in range(1, 4)]
    zls = [zl] + [lax.rem(zl + step, 4) for step in range(1, 4)]
    column = [(lows[a], zls[b], (dp - low + lows[a], zls[b])) for a in range(4) for b in range(4) if a or b]

    barrier = pltpu.get_barrier_semaphore()
    for index in range(15):
        for device in (plane[index][1], column[index][2]):
            pl.semaphore_signal(barrier, inc=1, device_id=device, device_id_type=MESH)

    def up_column(offset, which=None):
        zpos = lax.rem(z + offset, 8)
        return (xy * 4 + (zpos // 4) * 2 + (core if which is None else which), lax.rem(zpos, 4))

    def remote(src, dst, send, recv, device):
        return pltpu.make_async_remote_copy(
            src_ref=src, dst_ref=dst, send_sem=send, recv_sem=recv, device_id=device, device_id_type=MESH
        )

    loads = [
        pltpu.make_async_copy(win, win_v, load_sem.at[0]),
        pltpu.make_async_copy(qinp, qinp_v, load_sem.at[1]),
        pltpu.make_async_copy(wout, wout_v, load_sem.at[2]),
        pltpu.make_async_copy(qoutg, qoutg_v, load_sem.at[3]),
        pltpu.make_async_copy(ids_in, ids, load_sem.at[12]),
        pltpu.make_async_copy(qids_in, qids, load_sem.at[13]),
    ]
    owners = [zls[2], zls[1], zls[3], zl]
    chunk_loads = []
    for step in range(4):
        rows = pl.ds(pl.multiple_of(owners[step] * 128, 128), 128)
        chunk_loads.append(
            (
                pltpu.make_async_copy(inp.at[rows, :], inp_v.at[step], load_sem.at[4 + step]),
                pltpu.make_async_copy(outg.at[rows, :], outg_v.at[step], load_sem.at[8 + step]),
            )
        )
    def begin(some):
        for load in some:
            load.start()

    begin((loads[0], loads[2]))
    begin(chunk_loads[0])
    begin((loads[1], loads[3], loads[4], loads[5]))

    def project(left, right):
        return jnp.concatenate(
            [
                lax.dot_general(win_v[...], left, NT, preferred_element_type=F32),
                lax.dot_general(wout_v[...], right, NT, preferred_element_type=F32),
            ],
            axis=0,
        )

    def project_chunk(step):
        for load in chunk_loads[step]:
            load.wait()
        part[step] = project(inp_v[step], outg_v[step])

    pieces = [pl.ds(0, 32), pl.ds(32, 32), pl.ds(64, 32), pl.ds(96, 32)]
    rs_copies = [
        [
            remote(
                part.at[step, pieces[piece]], rs.at[zl, pieces[piece]], rs_send.at[step, piece],
                rs_recv.at[zl, piece], (dp, owners[step]),
            )
            for piece in range(4)
        ]
        for step in range(3)
    ]
    diag = lax.rem(xpos + ypos, 4)
    query_owner = jnp.where(core == 0, diag, 3 - diag)
    owns = zl == query_owner
    q_copy = remote(qpart, qrs.at[zl], q_send, q_recv.at[zl], (dp, query_owner))

    loads[0].wait()
    loads[2].wait()
    project_chunk(0)
    begin(chunk_loads[1])
    begin(chunk_loads[2])
    for index in (1, 3, 4, 5):
        loads[index].wait()
    qpart[...] = project(qinp_v[...], qoutg_v[...])
    begin(chunk_loads[3])
    project_chunk(1)
    pl.semaphore_wait(barrier, 30)
    for copy in rs_copies[0]:
        copy.start()

    @pl.when(jnp.logical_not(owns))
    def _():
        q_copy.start()

    for copy in rs_copies[1]:
        copy.start()
    project_chunk(2)
    for copy in rs_copies[2]:
        copy.start()
    project_chunk(3)
    rs[zl] = part[3]

    def first_done():
        @pl.when(jnp.logical_not(owns))
        def _():
            q_copy.wait_send()

        for copies in rs_copies:
            for copy in copies:
                copy.wait_send()

    pending.append(first_done)

    ids_own = jnp.zeros((1, 128), F32)
    for index in range(4):
        ids_own = ids_own + jnp.where(zl == index, ids[:, index * 128 : (index + 1) * 128].astype(F32), 0.0)
    own = z * 2 + core
    ft[own, 128:136] = jnp.broadcast_to(ids_own, (8, 128))

    whole = pl.ds(0, 129)
    pieces[3] = pl.ds(96, 33)
    halves = (pl.ds(0, 64), pl.ds(64, 65))
    sent = []

    def start(copy):
        copy.start()
        sent.append(copy)

    def handed(kind, piece, origin, target):
        where = ft.at[lax.rem(z + origin, 8) * 2 + core, pieces[piece], :]
        return remote(where, where, ag_send.at[kind, piece], ag_recv.at[kind, piece], up_column(target))

    def sibling(index, origin, rows, back=False):
        where = ft.at[lax.rem(z + origin, 8) * 2 + (1 - core if back else core), rows, :]
        return remote(where, where, sib_send.at[index], sib_recv.at[index], up_column(0, 1 - core))

    origins = (6, 2, 7, 1, 5, 3, 4, 4)

    def arrive(kind, piece):
        handed(kind, piece, origins[kind], 1).wait_recv()

    for piece in range(4):
        for step in range(1, 4):
            rows = pl.ds(piece * 32, 32)
            remote(
                part.at[0, rows], rs.at[zls[step], rows], rs_send.at[0, piece], rs_recv.at[zls[step], piece],
                (dp, zls[step]),
            ).wait_recv()
        span = slice(piece * 32, piece * 32 + 32)
        ft[own, span] = (rs[0, span] + rs[1, span]) + (rs[2, span] + rs[3, span])
        start(handed(0, piece, 0, 2))
        start(handed(1, piece, 0, 6))
    for piece in range(4):
        start(handed(2, piece, 0, 1))
        start(handed(3, piece, 0, 7))
    start(sibling(8, 0, whole))

    lane = lax.broadcasted_iota(jnp.int32, (128, 128), 1)
    pair_rows = pl.ds(pl.multiple_of(ypos * 64, 64), 64)
    b_copies = [
        remote(direction.at[pair_rows, :], direction.at[pair_rows, :], b_send.at[index], b_recv.at[ypos], device)
        for index, (_, device) in enumerate(plane)
    ]

    @pl.when(owns)
    def _():
        qrs[zl] = qpart[...]
        for step in range(1, 4):
            remote(qpart, qrs.at[zls[step]], q_send, q_recv.at[zls[step]], (dp, zls[step])).wait_recv()
        turned = (qrs[0] + qrs[1]) + (qrs[2] + qrs[3])
        feats = turned.T
        right = jnp.concatenate(
            [jnp.where(lane < 64, pltpu.roll(feats, 64, 1), 0.0), jnp.where(lane >= 64, feats, 0.0)], axis=0
        )
        rows = []
        for doc in range(2):
            mask = (qids[...] == doc).astype(F32)
            rows.append(jnp.concatenate([turned[0:32] * mask, turned[32:64] * mask], axis=1))
        direction[pair_rows, :] = jnp.dot(
            jnp.concatenate(rows, axis=0), right, precision=lax.Precision.HIGHEST, preferred_element_type=F32
        )
        for copy in b_copies:
            copy.start()

    for piece in range(4):
        arrive(0, piece)
        start(handed(4, piece, 6, 1))
        if piece < 2:
            start(handed(6, piece, 6, 2))
        arrive(1, piece)
        start(handed(5, piece, 2, 7))
        if piece >= 2:
            start(handed(7, piece, 2, 6))
    for kind in range(4):
        if kind >= 2:
            for piece in range(4):
                arrive(kind, piece)
        start(sibling(kind, origins[kind], whole))

    def prepare(tile):
        both = jnp.concatenate([ft[2 * tile], ft[2 * tile + 1]], axis=1)
        feat_a[tile] = both[0:64]
        high, rest = split_bf16(both[64:128])
        zero = jnp.zeros_like(high)
        rhs1[tile] = jnp.concatenate([high, high, rest, rest], axis=0)
        rhs2[tile] = jnp.concatenate(
            [
                jnp.concatenate([high, zero, rest, zero], axis=0),
                jnp.concatenate([zero, high, zero, rest], axis=0),
            ],
            axis=1,
        )

    near = [(8, 0), (0, 6), (1, 2), (2, 7), (3, 1)]
    for index, origin in near:
        sibling(index, origin, whole, True).wait_recv()
        prepare(lax.rem(z + origin, 8))
    far = [(4, 5, 0), (5, 3, 0), (6, 4, 0), (9, 5, 1), (10, 3, 1), (7, 4, 1)]
    for index, origin, side in far:
        kind = {5: 4, 3: 5, 4: 6 + side}[origin]
        for piece in (2 * side, 2 * side + 1):
            arrive(kind, piece)
        start(sibling(index, origin, halves[side]))

    for source in range(4):
        @pl.when(jnp.logical_not(jnp.logical_and(owns, ypos == source)))
        def _():
            rows = pl.ds(source * 64, 64)
            remote(
                direction.at[rows, :], direction.at[rows, :], b_send.at[0], b_recv.at[source], plane[0][1]
            ).wait_recv()

    lane_row = lax.broadcasted_iota(jnp.int32, (256, 128), 1)
    own_rows = pl.ds(pl.multiple_of(xy * 16, 16), 16)
    query_row = lax.broadcasted_iota(jnp.int32, (8, 1), 0)
    doc_row = lax.broadcasted_iota(jnp.int32, (128, 128), 0).astype(F32)

    def set_lhs(vector):
        high = vector.astype(BF16).astype(F32)
        rest = vector - high
        first = jnp.where(lane_row < 64, high, pltpu.roll(rest, 64, 1)).astype(BF16)
        second = jnp.where(lane_row < 64, pltpu.roll(high, 64, 1), rest).astype(BF16)
        lhs[0:256, 0:128] = first
        lhs[0:256, 128:256] = first
        lhs[256:512, 0:128] = second
        lhs[256:512, 128:256] = second

    def product(tile, squares, fresh, back):
        made = jnp.dot(lhs[...], rhs1[tile], preferred_element_type=F32)
        left = feat_a[tile].reshape(2, 1, 32, 256)
        inner = jnp.sum(jnp.sum(made.reshape(2, 8, 32, 256) * left, axis=0), axis=1)
        wbuf[tile] = inner
        if back:
            spread = (inner.reshape(1, 8, 1, 256) * left).reshape(2, 256, 256).astype(BF16)
            image = lax.dot_general(
                jnp.concatenate([spread[0], spread[1]], axis=1), rhs2[tile], NT, preferred_element_type=F32
            )
            if fresh:
                acc[...] = image
            else:
                acc[...] += image
        square = inner * inner
        return squares + square[:, 0:128] + square[:, 128:256]

    def document_sums():
        sums = []
        for group in range(4):
            side = pl.ds((group % 2) * 128, 128)
            tiles = [wbuf[(group // 2) * 4 + index, :, side] for index in range(4)]
            every = jnp.concatenate(tiles, axis=1)
            high = every.astype(BF16).astype(F32)
            both = jnp.concatenate([high, every - high], axis=0).astype(BF16)
            made = lax.dot_general(both, onehot[group], NT, preferred_element_type=F32)
            sums.append(made[0:8] + made[8:16])
        return sums

    def own_query(values):
        return jnp.sum(jnp.where(query_row == xy // 2, values, 0.0), axis=0, keepdims=True)

    message = pl.ds(0, 17)

    def send_all(copies):
        for copy in copies:
            copy.start()

    def sent_all(copies):
        for copy in copies:
            copy.wait_send()

    residual[...] = direction[...]
    norms = None
    scores = None
    for sweep in range(ITERS):
        last = sweep == ITERS - 1
        vector = direction[...]
        set_lhs(vector)
        squares = jnp.zeros((8, 128), F32)
        if sweep == 0:
            for place, (_, origin) in enumerate(near):
                squares = product(lax.rem(z + origin, 8), squares, place == 0, True)
            for index, origin, side in far:
                sibling(index, origin, halves[side], True).wait_recv()
            for origin in (5, 3, 4):
                prepare(lax.rem(z + origin, 8))
            for origin in (5, 3, 4):
                squares = product(lax.rem(z + origin, 8), squares, False, True)
        else:
            for tile in range(TILES):
                squares = product(tile, squares, tile == 0, not last)
        cube = vector.reshape(8, 32, 128)
        if not last:
            image = acc[:, 0:128] + acc[:, 128:256]
            usend[:, 0:16] = image.reshape(16, 16, 128)
            for index in range(16):
                usend[index, 16:17] = squares[index // 2 : index // 2 + 1]
            u_copies = [
                remote(usend.at[target, message], urecv.at[sweep, xy, message], u_send.at[sweep, index], u_recv.at[sweep, xy], device)
                for index, (target, device) in enumerate(plane)
            ]
            send_all(u_copies)
            urecv[sweep, xy, 0:17] = usend[xy, 0:17]
            if sweep == 0:
                for group in range(4):
                    for index in range(4):
                        chunk = ((group // 2) * 4 + index) * 2 + group % 2
                        onehot[group, :, index * 128 : (index + 1) * 128] = (doc_row == ft[chunk, 128:129]).astype(BF16)
            sums = document_sums()
            power = query_sum(cube * cube)
            if sweep == 0:
                norms = power
            for source, device in plane:
                remote(
                    usend.at[0, message], urecv.at[sweep, source, message], u_send.at[sweep, 0], u_recv.at[sweep, source], device
                ).wait_recv()
            total = jnp.sum(urecv[sweep, :, 0:17], axis=0)
            squared = jnp.sum(total[16:17], axis=1, keepdims=True)
            mine = own_query(norms) / (squared / tokens_all + DAMPING * own_query(power))
            own_image = total[0:16] / tokens_all + DAMPING * direction[own_rows, :]
            rbuf[sweep, xy, 0:16] = residual[own_rows, :] - mine * own_image
            rbuf[sweep, xy, 16:17] = jnp.broadcast_to(mine, (1, 128))
            r_copies = [
                remote(
                    rbuf.at[sweep, xy, message], rbuf.at[sweep, xy, message], r_send.at[sweep, index],
                    r_recv.at[sweep, xy], device,
                )
                for index, (_, device) in enumerate(plane)
            ]
            send_all(r_copies)
            pending.append(functools.partial(sent_all, r_copies))
            sent_all(u_copies)
            if sweep == 0:
                @pl.when(owns)
                def _():
                    sent_all(b_copies)

            for source, device in plane:
                remote(
                    rbuf.at[sweep, source, message], rbuf.at[sweep, source, message], r_send.at[sweep, 0],
                    r_recv.at[sweep, source], device,
                ).wait_recv()
            step_size = jnp.concatenate([rbuf[sweep, 2 * query, 16:17] for query in range(8)], axis=0)
            terms = [step_size * value for value in sums]
            scores = terms if scores is None else [a + b for a, b in zip(scores, terms)]
            left_over = rbuf[sweep, :, 0:16].reshape(256, 128)
            residual[...] = left_over
            cube_r = left_over.reshape(8, 32, 128)
            norms_next = query_sum(cube_r * cube_r)
            ratio = norms_next / norms
            direction[...] = (cube_r + ratio.reshape(8, 1, 1) * cube).reshape(256, 128)
            norms = norms_next

    ssend[...] = squares
    s_copies = [
        remote(ssend, srecv.at[xy], s_send.at[index], s_recv.at[xy], device)
        for index, (_, device) in enumerate(plane)
    ]
    send_all(s_copies)
    pending.append(functools.partial(sent_all, s_copies))
    srecv[xy] = squares
    power = query_sum(cube * cube)
    sums = document_sums()
    for source, device in plane:
        remote(ssend, srecv.at[source], s_send.at[0], s_recv.at[source], device).wait_recv()
    squared = jnp.sum(jnp.sum(srecv[...], axis=0), axis=1, keepdims=True)
    step_size = norms / (squared / tokens_all + DAMPING * power)

    for group in range(4):
        made = jnp.where(lane_row[0:8] < 16, (scores[group] + step_size * sums[group]) * (1.0 / 4096), 0.0)
        turned = [made[0:1]] + [pltpu.roll(made[query : query + 1], 16 * query, 1) for query in range(1, 8)]
        row = (turned[0] + turned[1]) + (turned[2] + turned[3]) + ((turned[4] + turned[5]) + (turned[6] + turned[7]))
        fsend[group, 0:1] = row

    def f_slot(where, height):
        return jnp.where(lax.rem(where, 2) == 0, height, 3 - height) * 4 + where

    own_slot = f_slot(low, zl)
    one_row = pl.ds(0, 1)
    f_copies = [
        remote(fsend.at[where, one_row], frecv.at[own_slot, one_row], f_send.at[index], f_recv.at[own_slot], device)
        for index, (where, _, device) in enumerate(column)
    ]
    send_all(f_copies)
    pending.append(functools.partial(sent_all, f_copies))
    frecv[own_slot, 0:1] = fsend[low, 0:1]
    for copy in sent:
        copy.wait_send()
    for done in pending:
        done()
    for where, height, device in column:
        slot = f_slot(where, height)
        remote(fsend.at[0, one_row], frecv.at[slot, one_row], f_send.at[0], f_recv.at[slot], device).wait_recv()
    for where in range(16):
        lined[where : where + 1] = frecv[where, 0:1]
    for query in range(8):
        row, which = query // 2, query % 2
        places = lined[...] if query == 0 else pltpu.roll(lined[...], 128 - 16 * query, 1)
        for diagonal in range(4):
            begin_row = row * 32 + ((diagonal - row) % 4) * 8 + which
            order[pl.ds(begin_row, 4, stride=2)] = places[4 * diagonal : 4 * diagonal + 4]
    out[...] = order[...].T[0:16]


def local(inputs, out_grads, query_inputs, query_grads, in_proj, out_proj, doc_ids, query_ids):
    tokens_all = inputs.shape[0] * lax.axis_size("dp")
    hbm = pl.BlockSpec(memory_space=pltpu.HBM)
    vmem = pl.BlockSpec(memory_space=pltpu.VMEM)
    dma = pltpu.SemaphoreType.DMA
    return pl.pallas_call(
        functools.partial(kernel, float(tokens_all)),
        out_shape=jax.ShapeDtypeStruct((16, 128), F32),
        in_specs=[hbm] * 8,
        out_specs=vmem,
        scratch_shapes=[
            pltpu.VMEM((1, 512), jnp.int32),
            pltpu.VMEM((1, 128), jnp.int32),
            pltpu.VMEM((64, 1280), BF16),
            pltpu.VMEM((64, 6912), BF16),
            pltpu.VMEM((4, 128, 1280), BF16),
            pltpu.VMEM((4, 128, 6912), BF16),
            pltpu.VMEM((128, 1280), BF16),
            pltpu.VMEM((128, 6912), BF16),
            pltpu.VMEM((4, 128, 128), F32),
            pltpu.VMEM((128, 128), F32),
            pltpu.VMEM((4, 128, 128), F32),
            pltpu.VMEM((4, 128, 128), F32),
            pltpu.VMEM((16, 136, 128), F32),
            pltpu.VMEM((TILES, 256, 256), BF16),
            pltpu.VMEM((TILES, 256, 512), BF16),
            pltpu.VMEM((TILES, 64, 256), F32),
            pltpu.VMEM((512, 256), BF16),
            pltpu.VMEM((TILES, 8, 256), F32),
            pltpu.VMEM((256, 256), F32),
            pltpu.VMEM((4, 128, 512), BF16),
            pltpu.VMEM((256, 128), F32),
            pltpu.VMEM((256, 128), F32),
            pltpu.VMEM((16, 24, 128), F32),
            pltpu.VMEM((2, 16, 24, 128), F32),
            pltpu.VMEM((2, 16, 24, 128), F32),
            pltpu.VMEM((8, 128), F32),
            pltpu.VMEM((16, 8, 128), F32),
            pltpu.VMEM((4, 8, 128), F32),
            pltpu.VMEM((16, 8, 128), F32),
            pltpu.VMEM((128, 128), F32),
            pltpu.VMEM((16, 128), F32),
            dma((14,)),
            dma((3, 4)),
            dma((4, 4)),
            dma,
            dma((4,)),
            dma((8, 4)),
            dma((8, 4)),
            dma((11,)),
            dma((11,)),
            dma((16,)),
            dma((4,)),
            dma((2, 16)),
            dma((2, 16)),
            dma((2, 16)),
            dma((2, 16)),
            dma((16,)),
            dma((16,)),
            dma((16,)),
            dma((16,)),
        ],
        compiler_params=pltpu.CompilerParams(
            collective_id=0, has_side_effects=True, vmem_limit_bytes=62 * 1024 * 1024
        ),
    )(inputs, out_grads, query_inputs, query_grads, in_proj.T, out_proj.T, doc_ids, query_ids)


def solution(mesh):
    return jax.shard_map(
        local,
        mesh=mesh,
        in_specs=(
            P("dp", "tensor"),
            P("dp", "tensor"),
            P("dp", "tensor"),
            P("dp", "tensor"),
            P("tensor", None),
            P("tensor", None),
            P("dp", None),
            P("dp", None),
        ),
        out_specs=P("dp", None),
        check_vma=False,
    )
```

```python
import functools

import jax
import jax.numpy as jnp
from jax import lax
from jax.experimental import pallas as pl
from jax.experimental.pallas import tpu as pltpu
from jax.sharding import PartitionSpec as P

MESH = pl.DeviceIdType.MESH
F32, BF16 = jnp.float32, jnp.bfloat16
NT = (((1,), (1,)), ((), ()))
ITERS = 3
DAMPING = 0.1
TILES = 8


def split_bf16(value):
    high = value.astype(BF16)
    return high, (value - high.astype(F32)).astype(BF16)


def query_sum(value):
    return jnp.sum(jnp.sum(value, axis=1), axis=1, keepdims=True)


def kernel(
    tokens_all,
    inp, outg, qinp, qoutg, win, wout, ids_in, qids_in,
    out,
    ids, qids, win_v, wout_v, inp_v, outg_v, qinp_v, qoutg_v,
    part, qpart, rs, qrs, ft, rhs1, rhs2, feat_a, lhs, wbuf, acc, onehot,
    direction, residual, usend, urecv, rbuf, ssend, srecv, fsend, frecv, order, lined,
    load_sem, rs_send, rs_recv, q_send, q_recv, ag_send, ag_recv, sib_send, sib_recv,
    b_send, b_recv, u_send, u_recv, r_send, r_recv, s_send, s_recv, f_send, f_recv,
):
    dp = lax.axis_index("dp")
    zl = lax.axis_index("tensor")
    low = lax.rem(dp, 4)
    core = lax.rem(dp, 2)
    half = low // 2
    xy = dp // 4
    xpos = lax.rem(xy, 4)
    ypos = xy // 4
    z = half * 4 + zl
    pending = []

    plane = [(lax.rem(xy + step, 16), (lax.rem(dp + 4 * step, 64), zl)) for step in range(1, 16)]
    lows = [low] + [lax.rem(low + step, 4) for step in range(1, 4)]
    zls = [zl] + [lax.rem(zl + step, 4) for step in range(1, 4)]
    column = [(lows[a], zls[b], (dp - low + lows[a], zls[b])) for a in range(4) for b in range(4) if a or b]

    barrier = pltpu.get_barrier_semaphore()
    for index in range(15):
        for device in (plane[index][1], column[index][2]):
            pl.semaphore_signal(barrier, inc=1, device_id=device, device_id_type=MESH)

    def up_column(offset, which=None):
        zpos = lax.rem(z + offset, 8)
        return (xy * 4 + (zpos // 4) * 2 + (core if which is None else which), lax.rem(zpos, 4))

    def remote(src, dst, send, recv, device):
        return pltpu.make_async_remote_copy(
            src_ref=src, dst_ref=dst, send_sem=send, recv_sem=recv, device_id=device, device_id_type=MESH
        )

    loads = [
        pltpu.make_async_copy(win, win_v, load_sem.at[0]),
        pltpu.make_async_copy(qinp, qinp_v, load_sem.at[1]),
        pltpu.make_async_copy(wout, wout_v, load_sem.at[2]),
        pltpu.make_async_copy(qoutg, qoutg_v, load_sem.at[3]),
        pltpu.make_async_copy(ids_in, ids, load_sem.at[12]),
        pltpu.make_async_copy(qids_in, qids, load_sem.at[13]),
    ]
    owners = [zls[2], zls[1], zls[3], zl]
    chunk_loads = []
    for step in range(4):
        rows = pl.ds(pl.multiple_of(owners[step] * 128, 128), 128)
        chunk_loads.append(
            (
                pltpu.make_async_copy(inp.at[rows, :], inp_v.at[step], load_sem.at[4 + step]),
                pltpu.make_async_copy(outg.at[rows, :], outg_v.at[step], load_sem.at[8 + step]),
            )
        )
    loads[0].start()
    loads[2].start()
    for pair in chunk_loads:
        for load in pair:
            load.start()
    for index in (1, 3, 4, 5):
        loads[index].start()

    def project(left, right):
        return jnp.concatenate(
            [
                lax.dot_general(win_v[...], left, NT, preferred_element_type=F32),
                lax.dot_general(wout_v[...], right, NT, preferred_element_type=F32),
            ],
            axis=0,
        )

    def project_chunk(step):
        for load in chunk_loads[step]:
            load.wait()
        part[step] = project(inp_v[step], outg_v[step])

    pieces = [pl.ds(0, 32), pl.ds(32, 32), pl.ds(64, 32), pl.ds(96, 32)]
    rs_copies = [
        [
            remote(
                part.at[step, pieces[piece]], rs.at[zl, pieces[piece]], rs_send.at[step, piece],
                rs_recv.at[zl, piece], (dp, owners[step]),
            )
            for piece in range(4)
        ]
        for step in range(3)
    ]
    diag = lax.rem(xpos + ypos, 4)
    query_owner = jnp.where(core == 0, diag, 3 - diag)
    owns = zl == query_owner
    q_copy = remote(qpart, qrs.at[zl], q_send, q_recv.at[zl], (dp, query_owner))

    loads[0].wait()
    loads[2].wait()
    project_chunk(0)
    project_chunk(1)
    pl.semaphore_wait(barrier, 30)
    for piece in range(4):
        rs_copies[0][piece].start()
        rs_copies[1][piece].start()
    project_chunk(2)
    for piece in range(4):
        rs_copies[2][piece].start()
    for index in (1, 3, 4, 5):
        loads[index].wait()
    qpart[...] = project(qinp_v[...], qoutg_v[...])

    @pl.when(jnp.logical_not(owns))
    def _():
        q_copy.start()

    project_chunk(3)
    rs[zl] = part[3]

    def first_done():
        @pl.when(jnp.logical_not(owns))
        def _():
            q_copy.wait_send()

        for copies in rs_copies:
            for copy in copies:
                copy.wait_send()

    pending.append(first_done)

    ids_own = jnp.zeros((1, 128), F32)
    for index in range(4):
        ids_own = ids_own + jnp.where(zl == index, ids[:, index * 128 : (index + 1) * 128].astype(F32), 0.0)
    own = z * 2 + core
    ft[own, 128:136] = jnp.broadcast_to(ids_own, (8, 128))

    whole = pl.ds(0, 129)
    pieces[3] = pl.ds(96, 33)
    halves = (pl.ds(0, 64), pl.ds(64, 65))
    sent = []

    def start(copy):
        copy.start()
        sent.append(copy)

    def handed(kind, piece, origin, target):
        where = ft.at[lax.rem(z + origin, 8) * 2 + core, pieces[piece], :]
        return remote(where, where, ag_send.at[kind, piece], ag_recv.at[kind, piece], up_column(target))

    def sibling(index, origin, rows, back=False):
        where = ft.at[lax.rem(z + origin, 8) * 2 + (1 - core if back else core), rows, :]
        return remote(where, where, sib_send.at[index], sib_recv.at[index], up_column(0, 1 - core))

    origins = (6, 2, 7, 1, 5, 3, 4, 4)

    def arrive(kind, piece):
        handed(kind, piece, origins[kind], 1).wait_recv()

    for piece in range(4):
        for step in range(1, 4):
            rows = pl.ds(piece * 32, 32)
            remote(
                part.at[0, rows], rs.at[zls[step], rows], rs_send.at[0, piece], rs_recv.at[zls[step], piece],
                (dp, zls[step]),
            ).wait_recv()
        span = slice(piece * 32, piece * 32 + 32)
        ft[own, span] = (rs[0, span] + rs[1, span]) + (rs[2, span] + rs[3, span])
        start(handed(0, piece, 0, 2))
        start(handed(1, piece, 0, 6))
    for piece in range(4):
        start(handed(2, piece, 0, 1))
        start(handed(3, piece, 0, 7))
    start(sibling(8, 0, whole))

    lane = lax.broadcasted_iota(jnp.int32, (128, 128), 1)
    pair_rows = pl.ds(pl.multiple_of(ypos * 64, 64), 64)
    b_copies = [
        remote(direction.at[pair_rows, :], direction.at[pair_rows, :], b_send.at[index], b_recv.at[ypos], device)
        for index, (_, device) in enumerate(plane)
    ]

    @pl.when(owns)
    def _():
        qrs[zl] = qpart[...]
        for step in range(1, 4):
            remote(qpart, qrs.at[zls[step]], q_send, q_recv.at[zls[step]], (dp, zls[step])).wait_recv()
        turned = (qrs[0] + qrs[1]) + (qrs[2] + qrs[3])
        feats = turned.T
        right = jnp.concatenate(
            [jnp.where(lane < 64, pltpu.roll(feats, 64, 1), 0.0), jnp.where(lane >= 64, feats, 0.0)], axis=0
        )
        rows = []
        for doc in range(2):
            mask = (qids[...] == doc).astype(F32)
            rows.append(jnp.concatenate([turned[0:32] * mask, turned[32:64] * mask], axis=1))
        direction[pair_rows, :] = jnp.dot(
            jnp.concatenate(rows, axis=0), right, precision=lax.Precision.HIGHEST, preferred_element_type=F32
        )
        for copy in b_copies:
            copy.start()

    for piece in range(4):
        arrive(0, piece)
        start(handed(4, piece, 6, 1))
        if piece < 2:
            start(handed(6, piece, 6, 2))
        arrive(1, piece)
        start(handed(5, piece, 2, 7))
        if piece >= 2:
            start(handed(7, piece, 2, 6))
    for kind in range(4):
        if kind >= 2:
            for piece in range(4):
                arrive(kind, piece)
        start(sibling(kind, origins[kind], whole))

    def prepare(tile):
        both = jnp.concatenate([ft[2 * tile], ft[2 * tile + 1]], axis=1)
        feat_a[tile] = both[0:64]
        high, rest = split_bf16(both[64:128])
        zero = jnp.zeros_like(high)
        rhs1[tile] = jnp.concatenate([high, high, rest, rest], axis=0)
        rhs2[tile] = jnp.concatenate(
            [
                jnp.concatenate([high, zero, rest, zero], axis=0),
                jnp.concatenate([zero, high, zero, rest], axis=0),
            ],
            axis=1,
        )

    near = [(8, 0), (0, 6), (1, 2), (2, 7), (3, 1)]
    for index, origin in near:
        sibling(index, origin, whole, True).wait_recv()
        prepare(lax.rem(z + origin, 8))
    far = [(4, 5, 0), (5, 3, 0), (6, 4, 0), (9, 5, 1), (10, 3, 1), (7, 4, 1)]
    for index, origin, side in far:
        kind = {5: 4, 3: 5, 4: 6 + side}[origin]
        for piece in (2 * side, 2 * side + 1):
            arrive(kind, piece)
        start(sibling(index, origin, halves[side]))

    for source in range(4):
        @pl.when(jnp.logical_not(jnp.logical_and(owns, ypos == source)))
        def _():
            rows = pl.ds(source * 64, 64)
            remote(
                direction.at[rows, :], direction.at[rows, :], b_send.at[0], b_recv.at[source], plane[0][1]
            ).wait_recv()

    lane_row = lax.broadcasted_iota(jnp.int32, (256, 128), 1)
    own_rows = pl.ds(pl.multiple_of(xy * 16, 16), 16)
    query_row = lax.broadcasted_iota(jnp.int32, (8, 1), 0)
    doc_row = lax.broadcasted_iota(jnp.int32, (128, 128), 0).astype(F32)

    def set_lhs(vector):
        high = vector.astype(BF16).astype(F32)
        rest = vector - high
        first = jnp.where(lane_row < 64, high, pltpu.roll(rest, 64, 1)).astype(BF16)
        second = jnp.where(lane_row < 64, pltpu.roll(high, 64, 1), rest).astype(BF16)
        lhs[0:256, 0:128] = first
        lhs[0:256, 128:256] = first
        lhs[256:512, 0:128] = second
        lhs[256:512, 128:256] = second

    def product(tile, squares, fresh, back):
        made = jnp.dot(lhs[...], rhs1[tile], preferred_element_type=F32)
        left = feat_a[tile].reshape(2, 1, 32, 256)
        inner = jnp.sum(jnp.sum(made.reshape(2, 8, 32, 256) * left, axis=0), axis=1)
        wbuf[tile] = inner
        if back:
            spread = (inner.reshape(1, 8, 1, 256) * left).reshape(2, 256, 256).astype(BF16)
            image = lax.dot_general(
                jnp.concatenate([spread[0], spread[1]], axis=1), rhs2[tile], NT, preferred_element_type=F32
            )
            if fresh:
                acc[...] = image
            else:
                acc[...] += image
        square = inner * inner
        return squares + square[:, 0:128] + square[:, 128:256]

    def document_sums():
        sums = []
        for group in range(4):
            side = pl.ds((group % 2) * 128, 128)
            tiles = [wbuf[(group // 2) * 4 + index, :, side] for index in range(4)]
            every = jnp.concatenate(tiles, axis=1)
            high = every.astype(BF16).astype(F32)
            both = jnp.concatenate([high, every - high], axis=0).astype(BF16)
            made = lax.dot_general(both, onehot[group], NT, preferred_element_type=F32)
            sums.append(made[0:8] + made[8:16])
        return sums

    def own_query(values):
        return jnp.sum(jnp.where(query_row == xy // 2, values, 0.0), axis=0, keepdims=True)

    message = pl.ds(0, 17)

    def send_all(copies):
        for copy in copies:
            copy.start()

    def sent_all(copies):
        for copy in copies:
            copy.wait_send()

    residual[...] = direction[...]
    norms = None
    every_sum = []
    for sweep in range(ITERS):
        last = sweep == ITERS - 1
        vector = direction[...]
        set_lhs(vector)
        squares = jnp.zeros((8, 128), F32)
        if sweep == 0:
            for place, (_, origin) in enumerate(near):
                squares = product(lax.rem(z + origin, 8), squares, place == 0, True)
            for index, origin, side in far:
                sibling(index, origin, halves[side], True).wait_recv()
            for origin in (5, 3, 4):
                prepare(lax.rem(z + origin, 8))
            for origin in (5, 3, 4):
                squares = product(lax.rem(z + origin, 8), squares, False, True)
        else:
            for tile in range(TILES):
                squares = product(tile, squares, tile == 0, not last)
        cube = vector.reshape(8, 32, 128)
        if not last:
            image = acc[:, 0:128] + acc[:, 128:256]
            usend[:, 0:16] = image.reshape(16, 16, 128)
            for index in range(16):
                usend[index, 16:17] = squares[index // 2 : index // 2 + 1]
            u_copies = [
                remote(usend.at[target, message], urecv.at[sweep, xy, message], u_send.at[sweep, index], u_recv.at[sweep, xy], device)
                for index, (target, device) in enumerate(plane)
            ]
            send_all(u_copies)
            urecv[sweep, xy, 0:17] = usend[xy, 0:17]
            if sweep == 0:
                for group in range(4):
                    for index in range(4):
                        chunk = ((group // 2) * 4 + index) * 2 + group % 2
                        onehot[group, :, index * 128 : (index + 1) * 128] = (doc_row == ft[chunk, 128:129]).astype(BF16)
            sums = document_sums()
            power = query_sum(cube * cube)
            if sweep == 0:
                norms = power
            for source, device in plane:
                remote(
                    usend.at[0, message], urecv.at[sweep, source, message], u_send.at[sweep, 0], u_recv.at[sweep, source], device
                ).wait_recv()
            total = jnp.sum(urecv[sweep, :, 0:17], axis=0)
            squared = jnp.sum(total[16:17], axis=1, keepdims=True)
            mine = own_query(norms) / (squared / tokens_all + DAMPING * own_query(power))
            own_image = total[0:16] / tokens_all + DAMPING * direction[own_rows, :]
            rbuf[sweep, xy, 0:16] = residual[own_rows, :] - mine * own_image
            rbuf[sweep, xy, 16:17] = jnp.broadcast_to(mine, (1, 128))
            r_copies = [
                remote(
                    rbuf.at[sweep, xy, message], rbuf.at[sweep, xy, message], r_send.at[sweep, index],
                    r_recv.at[sweep, xy], device,
                )
                for index, (_, device) in enumerate(plane)
            ]
            send_all(r_copies)
            pending.append(functools.partial(sent_all, r_copies))
            sent_all(u_copies)
            if sweep == 0:
                @pl.when(owns)
                def _():
                    sent_all(b_copies)

            for source, device in plane:
                remote(
                    rbuf.at[sweep, source, message], rbuf.at[sweep, source, message], r_send.at[sweep, 0],
                    r_recv.at[sweep, source], device,
                ).wait_recv()
            every_sum.append(sums)
            left_over = rbuf[sweep, :, 0:16].reshape(256, 128)
            residual[...] = left_over
            cube_r = left_over.reshape(8, 32, 128)
            norms_next = query_sum(cube_r * cube_r)
            ratio = norms_next / norms
            direction[...] = (cube_r + ratio.reshape(8, 1, 1) * cube).reshape(256, 128)
            norms = norms_next

    ssend[...] = squares
    s_copies = [
        remote(ssend, srecv.at[xy], s_send.at[index], s_recv.at[xy], device)
        for index, (_, device) in enumerate(plane)
    ]
    send_all(s_copies)
    pending.append(functools.partial(sent_all, s_copies))
    srecv[xy] = squares
    power = query_sum(cube * cube)
    sums = document_sums()
    scores = None
    for sweep in range(ITERS - 1):
        step_size = jnp.concatenate([rbuf[sweep, 2 * query, 16:17] for query in range(8)], axis=0)
        terms = [step_size * value for value in every_sum[sweep]]
        scores = terms if scores is None else [a + b for a, b in zip(scores, terms)]
    for source, device in plane:
        remote(ssend, srecv.at[source], s_send.at[0], s_recv.at[source], device).wait_recv()
    squared = jnp.sum(jnp.sum(srecv[...], axis=0), axis=1, keepdims=True)
    step_size = norms / (squared / tokens_all + DAMPING * power)

    for group in range(4):
        made = jnp.where(lane_row[0:8] < 16, (scores[group] + step_size * sums[group]) * (1.0 / 4096), 0.0)
        turned = [made[0:1]] + [pltpu.roll(made[query : query + 1], 16 * query, 1) for query in range(1, 8)]
        row = (turned[0] + turned[1]) + (turned[2] + turned[3]) + ((turned[4] + turned[5]) + (turned[6] + turned[7]))
        fsend[group, 0:1] = row

    def f_slot(where, height):
        return jnp.where(lax.rem(where, 2) == 0, height, 3 - height) * 4 + where

    own_slot = f_slot(low, zl)
    one_row = pl.ds(0, 1)
    f_copies = [
        remote(fsend.at[where, one_row], frecv.at[own_slot, one_row], f_send.at[index], f_recv.at[own_slot], device)
        for index, (where, _, device) in enumerate(column)
    ]
    send_all(f_copies)
    pending.append(functools.partial(sent_all, f_copies))
    frecv[own_slot, 0:1] = fsend[low, 0:1]
    for copy in sent:
        copy.wait_send()
    for done in pending:
        done()
    for where, height, device in column:
        slot = f_slot(where, height)
        remote(fsend.at[0, one_row], frecv.at[slot, one_row], f_send.at[0], f_recv.at[slot], device).wait_recv()
    for where in range(16):
        lined[where : where + 1] = frecv[where, 0:1]
    for query in range(8):
        row, which = query // 2, query % 2
        places = lined[...] if query == 0 else pltpu.roll(lined[...], 128 - 16 * query, 1)
        for diagonal in range(4):
            begin_row = row * 32 + ((diagonal - row) % 4) * 8 + which
            order[pl.ds(begin_row, 4, stride=2)] = places[4 * diagonal : 4 * diagonal + 4]
    out[...] = order[...].T[0:16]


def local(inputs, out_grads, query_inputs, query_grads, in_proj, out_proj, doc_ids, query_ids):
    tokens_all = inputs.shape[0] * lax.axis_size("dp")
    hbm = pl.BlockSpec(memory_space=pltpu.HBM)
    vmem = pl.BlockSpec(memory_space=pltpu.VMEM)
    dma = pltpu.SemaphoreType.DMA
    return pl.pallas_call(
        functools.partial(kernel, float(tokens_all)),
        out_shape=jax.ShapeDtypeStruct((16, 128), F32),
        in_specs=[hbm] * 8,
        out_specs=vmem,
        scratch_shapes=[
            pltpu.VMEM((1, 512), jnp.int32),
            pltpu.VMEM((1, 128), jnp.int32),
            pltpu.VMEM((64, 1280), BF16),
            pltpu.VMEM((64, 6912), BF16),
            pltpu.VMEM((4, 128, 1280), BF16),
            pltpu.VMEM((4, 128, 6912), BF16),
            pltpu.VMEM((128, 1280), BF16),
            pltpu.VMEM((128, 6912), BF16),
            pltpu.VMEM((4, 128, 128), F32),
            pltpu.VMEM((128, 128), F32),
            pltpu.VMEM((4, 128, 128), F32),
            pltpu.VMEM((4, 128, 128), F32),
            pltpu.VMEM((16, 136, 128), F32),
            pltpu.VMEM((TILES, 256, 256), BF16),
            pltpu.VMEM((TILES, 256, 512), BF16),
            pltpu.VMEM((TILES, 64, 256), F32),
            pltpu.VMEM((512, 256), BF16),
            pltpu.VMEM((TILES, 8, 256), F32),
            pltpu.VMEM((256, 256), F32),
            pltpu.VMEM((4, 128, 512), BF16),
            pltpu.VMEM((256, 128), F32),
            pltpu.VMEM((256, 128), F32),
            pltpu.VMEM((16, 24, 128), F32),
            pltpu.VMEM((2, 16, 24, 128), F32),
            pltpu.VMEM((2, 16, 24, 128), F32),
            pltpu.VMEM((8, 128), F32),
            pltpu.VMEM((16, 8, 128), F32),
            pltpu.VMEM((4, 8, 128), F32),
            pltpu.VMEM((16, 8, 128), F32),
            pltpu.VMEM((128, 128), F32),
            pltpu.VMEM((16, 128), F32),
            dma((14,)),
            dma((3, 4)),
            dma((4, 4)),
            dma,
            dma((4,)),
            dma((8, 4)),
            dma((8, 4)),
            dma((11,)),
            dma((11,)),
            dma((16,)),
            dma((4,)),
            dma((2, 16)),
            dma((2, 16)),
            dma((2, 16)),
            dma((2, 16)),
            dma((16,)),
            dma((16,)),
            dma((16,)),
            dma((16,)),
        ],
        compiler_params=pltpu.CompilerParams(
            collective_id=0, has_side_effects=True, vmem_limit_bytes=62 * 1024 * 1024
        ),
    )(inputs, out_grads, query_inputs, query_grads, in_proj.T, out_proj.T, doc_ids, query_ids)


def solution(mesh):
    return jax.shard_map(
        local,
        mesh=mesh,
        in_specs=(
            P("dp", "tensor"),
            P("dp", "tensor"),
            P("dp", "tensor"),
            P("dp", "tensor"),
            P("tensor", None),
            P("tensor", None),
            P("dp", None),
            P("dp", None),
        ),
        out_specs=P("dp", None),
        check_vma=False,
    )
```

```python
import functools

import jax
import jax.numpy as jnp
from jax import lax
from jax.experimental import pallas as pl
from jax.experimental.pallas import tpu as pltpu
from jax.sharding import PartitionSpec as P

MESH = pl.DeviceIdType.MESH
F32, BF16 = jnp.float32, jnp.bfloat16
NT = (((1,), (1,)), ((), ()))
ITERS = 3
DAMPING = 0.1
TILES = 8


def split_bf16(value):
    high = value.astype(BF16)
    return high, (value - high.astype(F32)).astype(BF16)


def query_sum(value):
    return jnp.sum(jnp.sum(value, axis=1), axis=1, keepdims=True)


def kernel(
    tokens_all,
    inp, outg, qinp, qoutg, win, wout, ids_in, qids_in,
    out,
    ids, qids, win_v, wout_v, inp_v, outg_v, qinp_v, qoutg_v,
    part, qpart, rs, qrs, ft, rhs1, rhs2, feat_a, lhs, wbuf, acc, onehot,
    direction, residual, usend, urecv, rbuf, ssend, srecv, fsend, frecv, order, lined,
    load_sem, rs_send, rs_recv, q_send, q_recv, ag_send, ag_recv, sib_send, sib_recv,
    b_send, b_recv, u_send, u_recv, r_send, r_recv, s_send, s_recv, f_send, f_recv,
):
    dp = lax.axis_index("dp")
    zl = lax.axis_index("tensor")
    low = lax.rem(dp, 4)
    core = lax.rem(dp, 2)
    half = low // 2
    xy = dp // 4
    xpos = lax.rem(xy, 4)
    ypos = xy // 4
    z = half * 4 + zl
    pending = []

    plane = [(lax.rem(xy + step, 16), (lax.rem(dp + 4 * step, 64), zl)) for step in range(1, 16)]
    lows = [low] + [lax.rem(low + step, 4) for step in range(1, 4)]
    zls = [zl] + [lax.rem(zl + step, 4) for step in range(1, 4)]
    column = [(lows[a], zls[b], (dp - low + lows[a], zls[b])) for a in range(4) for b in range(4) if a or b]

    barrier = pltpu.get_barrier_semaphore()
    for index in range(15):
        for device in (plane[index][1], column[index][2]):
            pl.semaphore_signal(barrier, inc=1, device_id=device, device_id_type=MESH)

    def up_column(offset, which=None):
        zpos = lax.rem(z + offset, 8)
        return (xy * 4 + (zpos // 4) * 2 + (core if which is None else which), lax.rem(zpos, 4))

    def remote(src, dst, send, recv, device):
        return pltpu.make_async_remote_copy(
            src_ref=src, dst_ref=dst, send_sem=send, recv_sem=recv, device_id=device, device_id_type=MESH
        )

    loads = [
        pltpu.make_async_copy(win, win_v, load_sem.at[0]),
        pltpu.make_async_copy(qinp, qinp_v, load_sem.at[1]),
        pltpu.make_async_copy(wout, wout_v, load_sem.at[2]),
        pltpu.make_async_copy(qoutg, qoutg_v, load_sem.at[3]),
        pltpu.make_async_copy(ids_in, ids, load_sem.at[12]),
        pltpu.make_async_copy(qids_in, qids, load_sem.at[13]),
    ]
    owners = [zls[2], zls[1], zls[3], zl]
    chunk_loads = []
    for step in range(4):
        rows = pl.ds(pl.multiple_of(owners[step] * 128, 128), 128)
        chunk_loads.append(
            (
                pltpu.make_async_copy(inp.at[rows, :], inp_v.at[step], load_sem.at[4 + step]),
                pltpu.make_async_copy(outg.at[rows, :], outg_v.at[step], load_sem.at[8 + step]),
            )
        )
    loads[0].start()
    loads[2].start()
    for pair in chunk_loads:
        for load in pair:
            load.start()
    for index in (1, 3, 4, 5):
        loads[index].start()

    def project(left, right):
        return jnp.concatenate(
            [
                lax.dot_general(win_v[...], left, NT, preferred_element_type=F32),
                lax.dot_general(wout_v[...], right, NT, preferred_element_type=F32),
            ],
            axis=0,
        )

    def project_chunk(step):
        for load in chunk_loads[step]:
            load.wait()
        part[step] = project(inp_v[step], outg_v[step])

    pieces = [pl.ds(0, 32), pl.ds(32, 32), pl.ds(64, 32), pl.ds(96, 32)]
    rs_copies = [
        [
            remote(
                part.at[step, pieces[piece]], rs.at[zl, pieces[piece]], rs_send.at[step, piece],
                rs_recv.at[zl, piece], (dp, owners[step]),
            )
            for piece in range(4)
        ]
        for step in range(3)
    ]
    diag = lax.rem(xpos + ypos, 4)
    query_owner = jnp.where(core == 0, diag, 3 - diag)
    owns = zl == query_owner
    q_copy = remote(qpart, qrs.at[zl], q_send, q_recv.at[zl], (dp, query_owner))

    loads[0].wait()
    loads[2].wait()
    project_chunk(0)
    project_chunk(1)
    pl.semaphore_wait(barrier, 30)
    for piece in range(4):
        rs_copies[0][piece].start()
        rs_copies[1][piece].start()
    project_chunk(2)
    for piece in range(4):
        rs_copies[2][piece].start()
    for index in (1, 3, 4, 5):
        loads[index].wait()
    qpart[...] = project(qinp_v[...], qoutg_v[...])

    @pl.when(jnp.logical_not(owns))
    def _():
        q_copy.start()

    project_chunk(3)
    rs[zl] = part[3]

    def first_done():
        @pl.when(jnp.logical_not(owns))
        def _():
            q_copy.wait_send()

        for copies in rs_copies:
            for copy in copies:
                copy.wait_send()

    pending.append(first_done)

    ids_own = jnp.zeros((1, 128), F32)
    for index in range(4):
        ids_own = ids_own + jnp.where(zl == index, ids[:, index * 128 : (index + 1) * 128].astype(F32), 0.0)
    own = z * 2 + core
    ft[own, 128:136] = jnp.broadcast_to(ids_own, (8, 128))

    whole = pl.ds(0, 129)
    pieces[3] = pl.ds(96, 33)
    halves = (pl.ds(0, 64), pl.ds(64, 65))
    sent = []

    def start(copy):
        copy.start()
        sent.append(copy)

    def handed(kind, piece, origin, target):
        where = ft.at[lax.rem(z + origin, 8) * 2 + core, pieces[piece], :]
        return remote(where, where, ag_send.at[kind, piece], ag_recv.at[kind, piece], up_column(target))

    def sibling(index, origin, rows, back=False):
        where = ft.at[lax.rem(z + origin, 8) * 2 + (1 - core if back else core), rows, :]
        return remote(where, where, sib_send.at[index], sib_recv.at[index], up_column(0, 1 - core))

    origins = (6, 2, 7, 1, 5, 3, 4, 4)

    def arrive(kind, piece):
        handed(kind, piece, origins[kind], 1).wait_recv()

    for piece in range(4):
        for step in range(1, 4):
            rows = pl.ds(piece * 32, 32)
            remote(
                part.at[0, rows], rs.at[zls[step], rows], rs_send.at[0, piece], rs_recv.at[zls[step], piece],
                (dp, zls[step]),
            ).wait_recv()
        span = slice(piece * 32, piece * 32 + 32)
        ft[own, span] = (rs[0, span] + rs[1, span]) + (rs[2, span] + rs[3, span])
        start(handed(0, piece, 0, 2))
        start(handed(1, piece, 0, 6))
    start(sibling(8, 0, whole))

    lane = lax.broadcasted_iota(jnp.int32, (128, 128), 1)
    pair_rows = pl.ds(pl.multiple_of(ypos * 64, 64), 64)
    b_copies = [
        remote(direction.at[pair_rows, :], direction.at[pair_rows, :], b_send.at[index], b_recv.at[ypos], device)
        for index, (_, device) in enumerate(plane)
    ]

    @pl.when(owns)
    def _():
        qrs[zl] = qpart[...]
        for step in range(1, 4):
            remote(qpart, qrs.at[zls[step]], q_send, q_recv.at[zls[step]], (dp, zls[step])).wait_recv()
        turned = (qrs[0] + qrs[1]) + (qrs[2] + qrs[3])
        feats = turned.T
        right = jnp.concatenate(
            [jnp.where(lane < 64, pltpu.roll(feats, 64, 1), 0.0), jnp.where(lane >= 64, feats, 0.0)], axis=0
        )
        rows = []
        for doc in range(2):
            mask = (qids[...] == doc).astype(F32)
            rows.append(jnp.concatenate([turned[0:32] * mask, turned[32:64] * mask], axis=1))
        direction[pair_rows, :] = jnp.dot(
            jnp.concatenate(rows, axis=0), right, precision=lax.Precision.HIGHEST, preferred_element_type=F32
        )
        for copy in b_copies:
            copy.start()

    for piece in range(4):
        arrive(0, piece)
        start(handed(4, piece, 6, 1))
        if piece < 2:
            start(handed(6, piece, 6, 2))
        arrive(1, piece)
        start(handed(5, piece, 2, 7))
        if piece >= 2:
            start(handed(7, piece, 2, 6))
        if piece == 0:
            for near_piece in range(4):
                start(handed(2, near_piece, 0, 1))
                start(handed(3, near_piece, 0, 7))
    for kind in range(4):
        if kind >= 2:
            for piece in range(4):
                arrive(kind, piece)
        start(sibling(kind, origins[kind], whole))

    def prepare(tile):
        both = jnp.concatenate([ft[2 * tile], ft[2 * tile + 1]], axis=1)
        feat_a[tile] = both[0:64]
        high, rest = split_bf16(both[64:128])
        zero = jnp.zeros_like(high)
        rhs1[tile] = jnp.concatenate([high, high, rest, rest], axis=0)
        rhs2[tile] = jnp.concatenate(
            [
                jnp.concatenate([high, zero, rest, zero], axis=0),
                jnp.concatenate([zero, high, zero, rest], axis=0),
            ],
            axis=1,
        )

    near = [(8, 0), (0, 6), (1, 2), (2, 7), (3, 1)]
    for index, origin in near:
        sibling(index, origin, whole, True).wait_recv()
        prepare(lax.rem(z + origin, 8))
    far = [(4, 5, 0), (5, 3, 0), (6, 4, 0), (9, 5, 1), (10, 3, 1), (7, 4, 1)]
    for index, origin, side in far:
        kind = {5: 4, 3: 5, 4: 6 + side}[origin]
        for piece in (2 * side, 2 * side + 1):
            arrive(kind, piece)
        start(sibling(index, origin, halves[side]))

    for source in range(4):
        @pl.when(jnp.logical_not(jnp.logical_and(owns, ypos == source)))
        def _():
            rows = pl.ds(source * 64, 64)
            remote(
                direction.at[rows, :], direction.at[rows, :], b_send.at[0], b_recv.at[source], plane[0][1]
            ).wait_recv()

    lane_row = lax.broadcasted_iota(jnp.int32, (256, 128), 1)
    own_rows = pl.ds(pl.multiple_of(xy * 16, 16), 16)
    query_row = lax.broadcasted_iota(jnp.int32, (8, 1), 0)
    doc_row = lax.broadcasted_iota(jnp.int32, (128, 128), 0).astype(F32)

    def set_lhs(vector):
        high = vector.astype(BF16).astype(F32)
        rest = vector - high
        first = jnp.where(lane_row < 64, high, pltpu.roll(rest, 64, 1)).astype(BF16)
        second = jnp.where(lane_row < 64, pltpu.roll(high, 64, 1), rest).astype(BF16)
        lhs[0:256, 0:128] = first
        lhs[0:256, 128:256] = first
        lhs[256:512, 0:128] = second
        lhs[256:512, 128:256] = second

    def product(tile, squares, fresh, back):
        made = jnp.dot(lhs[...], rhs1[tile], preferred_element_type=F32)
        left = feat_a[tile].reshape(2, 1, 32, 256)
        inner = jnp.sum(jnp.sum(made.reshape(2, 8, 32, 256) * left, axis=0), axis=1)
        wbuf[tile] = inner
        if back:
            spread = (inner.reshape(1, 8, 1, 256) * left).reshape(2, 256, 256).astype(BF16)
            image = lax.dot_general(
                jnp.concatenate([spread[0], spread[1]], axis=1), rhs2[tile], NT, preferred_element_type=F32
            )
            if fresh:
                acc[...] = image
            else:
                acc[...] += image
        square = inner * inner
        return squares + square[:, 0:128] + square[:, 128:256]

    def document_sums():
        sums = []
        for group in range(4):
            side = pl.ds((group % 2) * 128, 128)
            tiles = [wbuf[(group // 2) * 4 + index, :, side] for index in range(4)]
            every = jnp.concatenate(tiles, axis=1)
            high = every.astype(BF16).astype(F32)
            both = jnp.concatenate([high, every - high], axis=0).astype(BF16)
            made = lax.dot_general(both, onehot[group], NT, preferred_element_type=F32)
            sums.append(made[0:8] + made[8:16])
        return sums

    def own_query(values):
        return jnp.sum(jnp.where(query_row == xy // 2, values, 0.0), axis=0, keepdims=True)

    message = pl.ds(0, 17)

    def send_all(copies):
        for copy in copies:
            copy.start()

    def sent_all(copies):
        for copy in copies:
            copy.wait_send()

    residual[...] = direction[...]
    norms = None
    every_sum = []
    for sweep in range(ITERS):
        last = sweep == ITERS - 1
        vector = direction[...]
        set_lhs(vector)
        squares = jnp.zeros((8, 128), F32)
        if sweep == 0:
            for place, (_, origin) in enumerate(near):
                squares = product(lax.rem(z + origin, 8), squares, place == 0, True)
            for index, origin, side in far:
                sibling(index, origin, halves[side], True).wait_recv()
            for origin in (5, 3, 4):
                prepare(lax.rem(z + origin, 8))
            for origin in (5, 3, 4):
                squares = product(lax.rem(z + origin, 8), squares, False, True)
        else:
            for tile in range(TILES):
                squares = product(tile, squares, tile == 0, not last)
        cube = vector.reshape(8, 32, 128)
        if not last:
            image = acc[:, 0:128] + acc[:, 128:256]
            usend[:, 0:16] = image.reshape(16, 16, 128)
            for index in range(16):
                usend[index, 16:17] = squares[index // 2 : index // 2 + 1]
            u_copies = [
                remote(usend.at[target, message], urecv.at[sweep, xy, message], u_send.at[sweep, index], u_recv.at[sweep, xy], device)
                for index, (target, device) in enumerate(plane)
            ]
            send_all(u_copies)
            urecv[sweep, xy, 0:17] = usend[xy, 0:17]
            if sweep == 0:
                for group in range(4):
                    for index in range(4):
                        chunk = ((group // 2) * 4 + index) * 2 + group % 2
                        onehot[group, :, index * 128 : (index + 1) * 128] = (doc_row == ft[chunk, 128:129]).astype(BF16)
            sums = document_sums()
            power = query_sum(cube * cube)
            if sweep == 0:
                norms = power
            for source, device in plane:
                remote(
                    usend.at[0, message], urecv.at[sweep, source, message], u_send.at[sweep, 0], u_recv.at[sweep, source], device
                ).wait_recv()
            total = jnp.sum(urecv[sweep, :, 0:17], axis=0)
            squared = jnp.sum(total[16:17], axis=1, keepdims=True)
            mine = own_query(norms) / (squared / tokens_all + DAMPING * own_query(power))
            own_image = total[0:16] / tokens_all + DAMPING * direction[own_rows, :]
            rbuf[sweep, xy, 0:16] = residual[own_rows, :] - mine * own_image
            rbuf[sweep, xy, 16:17] = jnp.broadcast_to(mine, (1, 128))
            r_copies = [
                remote(
                    rbuf.at[sweep, xy, message], rbuf.at[sweep, xy, message], r_send.at[sweep, index],
                    r_recv.at[sweep, xy], device,
                )
                for index, (_, device) in enumerate(plane)
            ]
            send_all(r_copies)
            pending.append(functools.partial(sent_all, r_copies))
            sent_all(u_copies)
            if sweep == 0:
                @pl.when(owns)
                def _():
                    sent_all(b_copies)

            for source, device in plane:
                remote(
                    rbuf.at[sweep, source, message], rbuf.at[sweep, source, message], r_send.at[sweep, 0],
                    r_recv.at[sweep, source], device,
                ).wait_recv()
            every_sum.append(sums)
            left_over = rbuf[sweep, :, 0:16].reshape(256, 128)
            residual[...] = left_over
            cube_r = left_over.reshape(8, 32, 128)
            norms_next = query_sum(cube_r * cube_r)
            ratio = norms_next / norms
            direction[...] = (cube_r + ratio.reshape(8, 1, 1) * cube).reshape(256, 128)
            norms = norms_next

    ssend[...] = squares
    s_copies = [
        remote(ssend, srecv.at[xy], s_send.at[index], s_recv.at[xy], device)
        for index, (_, device) in enumerate(plane)
    ]
    send_all(s_copies)
    pending.append(functools.partial(sent_all, s_copies))
    srecv[xy] = squares
    power = query_sum(cube * cube)
    sums = document_sums()
    scores = None
    for sweep in range(ITERS - 1):
        step_size = jnp.concatenate([rbuf[sweep, 2 * query, 16:17] for query in range(8)], axis=0)
        terms = [step_size * value for value in every_sum[sweep]]
        scores = terms if scores is None else [a + b for a, b in zip(scores, terms)]
    for source, device in plane:
        remote(ssend, srecv.at[source], s_send.at[0], s_recv.at[source], device).wait_recv()
    squared = jnp.sum(jnp.sum(srecv[...], axis=0), axis=1, keepdims=True)
    step_size = norms / (squared / tokens_all + DAMPING * power)

    for group in range(4):
        made = jnp.where(lane_row[0:8] < 16, (scores[group] + step_size * sums[group]) * (1.0 / 4096), 0.0)
        turned = [made[0:1]] + [pltpu.roll(made[query : query + 1], 16 * query, 1) for query in range(1, 8)]
        row = (turned[0] + turned[1]) + (turned[2] + turned[3]) + ((turned[4] + turned[5]) + (turned[6] + turned[7]))
        fsend[group, 0:1] = row

    def f_slot(where, height):
        return jnp.where(lax.rem(where, 2) == 0, height, 3 - height) * 4 + where

    own_slot = f_slot(low, zl)
    one_row = pl.ds(0, 1)
    f_copies = [
        remote(fsend.at[where, one_row], frecv.at[own_slot, one_row], f_send.at[index], f_recv.at[own_slot], device)
        for index, (where, _, device) in enumerate(column)
    ]
    send_all(f_copies)
    pending.append(functools.partial(sent_all, f_copies))
    frecv[own_slot, 0:1] = fsend[low, 0:1]
    for copy in sent:
        copy.wait_send()
    for done in pending:
        done()
    for where, height, device in column:
        slot = f_slot(where, height)
        remote(fsend.at[0, one_row], frecv.at[slot, one_row], f_send.at[0], f_recv.at[slot], device).wait_recv()
    for where in range(16):
        lined[where : where + 1] = frecv[where, 0:1]
    for query in range(8):
        row, which = query // 2, query % 2
        places = lined[...] if query == 0 else pltpu.roll(lined[...], 128 - 16 * query, 1)
        for diagonal in range(4):
            begin_row = row * 32 + ((diagonal - row) % 4) * 8 + which
            order[pl.ds(begin_row, 4, stride=2)] = places[4 * diagonal : 4 * diagonal + 4]
    out[...] = order[...].T[0:16]


def local(inputs, out_grads, query_inputs, query_grads, in_proj, out_proj, doc_ids, query_ids):
    tokens_all = inputs.shape[0] * lax.axis_size("dp")
    hbm = pl.BlockSpec(memory_space=pltpu.HBM)
    vmem = pl.BlockSpec(memory_space=pltpu.VMEM)
    dma = pltpu.SemaphoreType.DMA
    return pl.pallas_call(
        functools.partial(kernel, float(tokens_all)),
        out_shape=jax.ShapeDtypeStruct((16, 128), F32),
        in_specs=[hbm] * 8,
        out_specs=vmem,
        scratch_shapes=[
            pltpu.VMEM((1, 512), jnp.int32),
            pltpu.VMEM((1, 128), jnp.int32),
            pltpu.VMEM((64, 1280), BF16),
            pltpu.VMEM((64, 6912), BF16),
            pltpu.VMEM((4, 128, 1280), BF16),
            pltpu.VMEM((4, 128, 6912), BF16),
            pltpu.VMEM((128, 1280), BF16),
            pltpu.VMEM((128, 6912), BF16),
            pltpu.VMEM((4, 128, 128), F32),
            pltpu.VMEM((128, 128), F32),
            pltpu.VMEM((4, 128, 128), F32),
            pltpu.VMEM((4, 128, 128), F32),
            pltpu.VMEM((16, 136, 128), F32),
            pltpu.VMEM((TILES, 256, 256), BF16),
            pltpu.VMEM((TILES, 256, 512), BF16),
            pltpu.VMEM((TILES, 64, 256), F32),
            pltpu.VMEM((512, 256), BF16),
            pltpu.VMEM((TILES, 8, 256), F32),
            pltpu.VMEM((256, 256), F32),
            pltpu.VMEM((4, 128, 512), BF16),
            pltpu.VMEM((256, 128), F32),
            pltpu.VMEM((256, 128), F32),
            pltpu.VMEM((16, 24, 128), F32),
            pltpu.VMEM((2, 16, 24, 128), F32),
            pltpu.VMEM((2, 16, 24, 128), F32),
            pltpu.VMEM((8, 128), F32),
            pltpu.VMEM((16, 8, 128), F32),
            pltpu.VMEM((4, 8, 128), F32),
            pltpu.VMEM((16, 8, 128), F32),
            pltpu.VMEM((128, 128), F32),
            pltpu.VMEM((16, 128), F32),
            dma((14,)),
            dma((3, 4)),
            dma((4, 4)),
            dma,
            dma((4,)),
            dma((8, 4)),
            dma((8, 4)),
            dma((11,)),
            dma((11,)),
            dma((16,)),
            dma((4,)),
            dma((2, 16)),
            dma((2, 16)),
            dma((2, 16)),
            dma((2, 16)),
            dma((16,)),
            dma((16,)),
            dma((16,)),
            dma((16,)),
        ],
        compiler_params=pltpu.CompilerParams(
            collective_id=0, has_side_effects=True, vmem_limit_bytes=62 * 1024 * 1024
        ),
    )(inputs, out_grads, query_inputs, query_grads, in_proj.T, out_proj.T, doc_ids, query_ids)


def solution(mesh):
    return jax.shard_map(
        local,
        mesh=mesh,
        in_specs=(
            P("dp", "tensor"),
            P("dp", "tensor"),
            P("dp", "tensor"),
            P("dp", "tensor"),
            P("tensor", None),
            P("tensor", None),
            P("dp", None),
            P("dp", None),
        ),
        out_specs=P("dp", None),
        check_vma=False,
    )
```
